256 devices in a mesh: strip: 64 (over x, z, core), sub: 4 (over y).
Axes of the slice: x: 4, y: 4, z: 8, core: 2. Of those that a mesh axis runs over, the one named last changes fastest.
Arguments:
- amplitudes: bfloat16 [128, 128, 128, 128], P('strip', 'sub'), may hold values from -6 to 6
- tno_size: int32 [128], P('strip'), may hold values from 64 to 128, as said below
- pair_amps: bfloat16 [1536, 128, 128], P('strip', 'sub'), may hold values from -0.5 to 0.5
- integrals: bfloat16 [128, 3, 128, 128, 128], P('strip', None, 'sub'), may hold values from -6 to 6
- pair_intersection: bfloat16 [128, 3, 128, 128], P('strip')
- nbr_intersection: bfloat16 [128, 3, 128, 128], P('strip')
- tno_energy: float32 [128, 128], P('strip'), may hold values from 0.3 to 3
- lmo_energy: float32 [3000], replicated, may hold values from -1.2 to -0.2
- triples: int32 [128, 3], P('strip'), may hold values from 0 to 2999
- pair_ids: int32 [128, 3], P('strip'), may hold values from 0 to 1535, as said below
- nbr_ids: int32 [128, 3], P('strip'), may hold values from 0 to 127, as said below
- nbr_fock: float32 [128, 3], P('strip'), may hold values from -2 to 2
Outputs:
- new_amplitudes: bfloat16 [128, 128, 128, 128], P('strip', 'sub')
The draws below stay inside these ranges and needn't reach their ends.
Inputs may be any that keep to these rules, and one draw needn't show every extreme that they name: `tno_size`: at least one triple has 128 live TNO functions. `pair_ids`: pair p is owned by strip p // 24; triple t by strip t // 2. The triples of one strip name at most 2 pairs owned by any one strip, counted with repeats, and exactly 2 of at least one owner; the three pairs of a triple are distinct. `nbr_ids`: every neighbour triple belongs to the strip just below or just above the triple's own strip, never to the same strip.
All inputs are finite; a program needn't handle non-finite values.
Results may differ from the reference program's by a relative error of at most 0.007.
Values may be sent and summed in bfloat16 or wider, within the bound.
A program may use at most 192 MiB of HBM per device.

```python
import math
import jax
import jax.numpy as jnp
from jax import lax

NT = 128
NP = 128
NLMO = 3000
NB = 3
CAP = 2
TRI_STRIP = 2
PAIR_STRIP = 24
TRIPLES = 128
PAIRS = 1536


def draw_tno_size(key, part):
    key = jax.random.fold_in(key, 17)
    values = jax.random.randint(key, (TRIPLES,), NT // 2, NT + 1)
    return values.at[0].set(NT).astype(jnp.int32)


def draw_pair_intersection(key, part):
    key = jax.random.fold_in(key, 5)
    noise = jax.random.normal(key, (TRIPLES, 3, NT, NP), jnp.float32)
    return (0.9 * jnp.eye(NT, NP, dtype=jnp.float32) + 0.4 * noise / math.sqrt(NP)).astype(jnp.bfloat16)


def draw_nbr_intersection(key, part):
    key = jax.random.fold_in(key, 7)
    noise = jax.random.normal(key, (TRIPLES, NB, NT, NT), jnp.float32)
    return (0.9 * jnp.eye(NT, NT, dtype=jnp.float32) + 0.4 * noise / math.sqrt(NT)).astype(jnp.bfloat16)


def draw_pair_ids(key, part):
    key = jax.random.fold_in(key, 11)
    strips = TRIPLES // TRI_STRIP
    wanted = 3 * TRI_STRIP
    key_owner, key_order, key_slot = jax.random.split(key, 3)
    owner_perm = jax.vmap(lambda k: jax.random.permutation(k, strips))(jax.random.split(key_owner, strips))
    order = jax.vmap(lambda k: jax.random.permutation(k, wanted))(jax.random.split(key_order, strips))
    groups = order // CAP
    owners = jnp.take_along_axis(owner_perm, groups, axis=1)
    base = jax.random.randint(key_slot, (strips, wanted), 0, PAIR_STRIP)
    base_group = jnp.take_along_axis(base, groups, axis=1)
    slots = (base_group + order % CAP) % PAIR_STRIP
    return (owners * PAIR_STRIP + slots).reshape(TRIPLES, 3).astype(jnp.int32)


def draw_nbr_ids(key, part):
    key = jax.random.fold_in(key, 13)
    strips = TRIPLES // TRI_STRIP
    key_side, key_local = jax.random.split(key)
    home = (jnp.arange(TRIPLES, dtype=jnp.int32) // TRI_STRIP)[:, None]
    side = jax.random.randint(key_side, (TRIPLES, NB), 0, 2) * 2 - 1
    side = jnp.where(home == 0, 1, jnp.where(home == strips - 1, -1, side))
    local = jax.random.randint(key_local, (TRIPLES, NB), 0, TRI_STRIP)
    return ((home + side) * TRI_STRIP + local).astype(jnp.int32)


def place_ends(values, stream_key, smallest, largest):
    place = [jax.random.randint(jax.random.fold_in(stream_key, axis), (), 0, length) for axis, length in enumerate(values.shape)]
    longest = values.shape.index(max(values.shape))
    next_to = place[:longest] + [(place[longest] + 1) % values.shape[longest]] + place[longest + 1:]
    return values.at[tuple(place)].set(smallest).at[tuple(next_to)].set(largest)


def levels(rng, dims, shards, low, largest):
    level = 1.0
    for dim, blocks in shards:
        steps = jax.random.uniform(jax.random.fold_in(jax.random.fold_in(rng, 6), dim), (blocks,), jnp.float32, low / len(shards), largest / len(shards))
        level = level * jnp.repeat(jnp.exp(steps), dims[dim] // blocks).reshape((-1,) + (1,) * (len(dims) - 1 - dim))
    return level


def scatter_about(key, shape, width, reach, cuts=(), held_as=jnp.bfloat16):
    loudness = levels(key, shape, cuts, -0.22, 0.18) if cuts else 1.0
    drawn = jax.random.normal(key, shape, jnp.float32) * width * loudness
    return jnp.minimum(jnp.maximum(drawn, -reach), reach).astype(held_as)


def setup_inputs(seed: int = 0) -> dict:
    arg_keys = jax.random.split(jax.random.key(seed), 13)
    return {
        "amplitudes": scatter_about(arg_keys[0], (TRIPLES, NT, NT, NT), 1.0, 6.0, ((0, 64), (1, 4))),
        "tno_size": draw_tno_size(jax.random.fold_in(arg_keys[12], 71), 0),
        "pair_amps": scatter_about(arg_keys[2], (PAIRS, NP, NP), NP ** -0.5, 0.5, ((0, 64), (1, 4))),
        "integrals": scatter_about(arg_keys[3], (TRIPLES, 3, NT, NT, NT), 1.0, 6.0, ((0, 64), (2, 4))),
        "pair_intersection": draw_pair_intersection(jax.random.fold_in(arg_keys[12], 71), 0),
        "nbr_intersection": draw_nbr_intersection(jax.random.fold_in(arg_keys[12], 71), 0),
        "tno_energy": jnp.clip(jnp.exp(math.log(3.0) - 2.3025851 * jax.random.uniform(arg_keys[6], (TRIPLES, NT), jnp.float32) ** levels(arg_keys[6], (TRIPLES, NT), ((0, 64),), -0.2, 0.2)), 0.3, 3.0),
        "lmo_energy": jnp.clip(jax.random.uniform(arg_keys[7], (NLMO,), jnp.float32, -1.2, -0.2), -1.2, -0.2),
        "triples": place_ends(jax.random.randint(arg_keys[8], (TRIPLES, 3), 0, NLMO), jax.random.fold_in(arg_keys[8], 1), 0, NLMO - 1).astype(jnp.int32),
        "pair_ids": draw_pair_ids(jax.random.fold_in(arg_keys[12], 71), 0),
        "nbr_ids": draw_nbr_ids(jax.random.fold_in(arg_keys[12], 71), 0),
        "nbr_fock": scatter_about(arg_keys[11], (TRIPLES, NB), 0.6, 2.0, ((0, 64),), jnp.float32),
    }


def reference(amplitudes, tno_size, pair_amps, integrals, pair_intersection, nbr_intersection, tno_energy, lmo_energy, triples, pair_ids, nbr_ids, nbr_fock):
    positions = jnp.arange(NT)
    inside = positions[None, :] < tno_size[:, None]
    support = inside[:, :, None, None] & inside[:, None, :, None] & inside[:, None, None, :]
    masked = jnp.where(support, amplitudes, jnp.zeros((), jnp.bfloat16))
    blocks = pair_amps[pair_ids].astype(jnp.float32)
    pair_over = pair_intersection.astype(jnp.float32)
    left_half = jnp.einsum('trax,trxy->tray', pair_over, blocks).astype(jnp.bfloat16)
    pair_tno = jnp.einsum('tray,trdy->trad', left_half.astype(jnp.float32), pair_over).astype(jnp.bfloat16)
    lmo_total = jnp.sum(lmo_energy[triples], axis=1)

    def update_triple(t):
        wsum = jnp.einsum('rad,rcdb->cab', pair_tno[t].astype(jnp.float32), integrals[t].astype(jnp.float32))
        wsum = wsum + jnp.transpose(wsum, (0, 2, 1))
        neighbours = masked[nbr_ids[t]].astype(jnp.float32)
        intersection_t = nbr_intersection[t].astype(jnp.float32)
        half_proj = jnp.einsum('nzxy,nax->nzya', neighbours, intersection_t).astype(jnp.bfloat16)
        projected = jnp.einsum('nzya,nby->nzab', half_proj.astype(jnp.float32), intersection_t).astype(jnp.bfloat16)
        coupled = jnp.einsum('n,ncz,nzab->cab', nbr_fock[t], intersection_t, projected.astype(jnp.float32))
        energy = tno_energy[t]
        denominator = energy[:, None, None] + energy[None, :, None] + energy[None, None, :] - lmo_total[t]
        current = masked[t].astype(jnp.float32)
        residual = wsum + denominator * current - coupled
        result = current - 0.7 * residual / denominator
        return jnp.where(support[t], result, jnp.float32(0.0)).astype(jnp.bfloat16)

    return lax.map(update_triple, jnp.arange(TRIPLES))
```

```python
import functools

import jax
import jax.numpy as jnp
from jax import lax
from jax.experimental import pallas as pl
from jax.experimental.pallas import tpu as pltpu
from jax.sharding import PartitionSpec as P

MESH = pl.DeviceIdType.MESH
F32 = jnp.float32
BF16 = jnp.bfloat16
ZP = 4
AP = 4
CAP = 2


def kernel(
    strips, subs, tri, nbrs, share, width, owned,
    size_ref, pair_ids_ref, nbr_ids_ref, fock_ref, triples_ref, lmo_ref, energy_ref,
    energy_rows_ref, amp_ref, pairs_ref, ints_ref, over_ref, inter_ref,
    out_ref,
    held0, held1, held2, held3, pbuf, part, recv, ints, amp, pairs, over, s_raw, s_mask, w_all,
    masks_out, masks_in, ids_out, ids_all, ids_smem, staging, got, mine, blocks,
    local_sem, mask_send, mask_recv, ids_sem, ids_send, ids_recv, shift_send, shift_recv,
    pair_send, pair_recv, rows_send, rows_recv, ring_send, ring_recv,
):
    strip = lax.axis_index("strip")
    sub = lax.axis_index("sub")
    up = lax.rem(strip + 1, strips)
    down = lax.rem(strip + strips - 1, strips)
    zs = share // ZP
    rows_p = width // 2 // AP
    k = nbrs * share
    wants = tri * 3
    flat = tri * share * width

    held = (held0, held1, held2, held3)
    loads = [
        pltpu.make_async_copy(src, dst, local_sem.at[i])
        for i, (src, dst) in enumerate(
            [(inter_ref, s_raw), (pairs_ref, pairs), (over_ref, over), (amp_ref, amp), (ints_ref, ints)]
        )
    ]
    for copy in loads:
        copy.start()

    barrier = pltpu.get_barrier_semaphore()

    def greet(i, carry):
        other = lax.rem(strip + i, strips)
        pl.semaphore_signal(barrier, inc=1, device_id=(other, sub), device_id_type=MESH)
        return carry

    lax.fori_loop(1, strips, greet, 0)
    for i in range(1, subs):
        pl.semaphore_signal(
            barrier, inc=1, device_id=(strip, lax.rem(sub + i, subs)), device_id_type=MESH
        )

    lane = lax.broadcasted_iota(jnp.int32, (1, width), 1)
    for t in range(tri):
        size = size_ref[t]
        masks_out[t, 0:1] = jnp.where(lane < size, 1.0, 0.0).astype(F32)
        masks_out[t, 1:2] = jnp.where(lax.rem(lane, share) + sub * share < size, 1.0, 0.0).astype(F32)
        masks_out[t, 2:8] = jnp.zeros((6, width), F32)
    row = jnp.zeros((1, width), jnp.int32)
    for r in range(wants):
        row = jnp.where(lane == r, pair_ids_ref[r // 3, r % 3], row)
    ids_out[...] = row
    pl.semaphore_wait(barrier, strips + subs - 2)

    def mask_copy(side):
        return pltpu.make_async_remote_copy(
            src_ref=masks_out,
            dst_ref=masks_in.at[pl.ds(side * tri, tri)],
            send_sem=mask_send.at[side],
            recv_sem=mask_recv.at[side],
            device_id=((up if side == 0 else down), sub),
            device_id_type=MESH,
        )

    def shift(side, j):
        return pltpu.make_async_remote_copy(
            src_ref=amp_ref.at[:, pl.ds(j * zs, zs)],
            dst_ref=held[j].at[pl.ds(side * tri, tri)],
            send_sem=shift_send.at[side, j],
            recv_sem=shift_recv.at[side, j],
            device_id=((up if side == 0 else down), sub),
            device_id_type=MESH,
        )

    def ids_copy(i, origin):
        return pltpu.make_async_remote_copy(
            src_ref=ids_out,
            dst_ref=ids_all.at[origin],
            send_sem=ids_send.at[i],
            recv_sem=ids_recv.at[origin],
            device_id=(lax.rem(strip + i, strips), sub),
            device_id_type=MESH,
        )

    def pair_copy(i, origin):
        other = lax.rem(strip + i, strips)
        return pltpu.make_async_remote_copy(
            src_ref=staging.at[other],
            dst_ref=got.at[origin],
            send_sem=pair_send.at[i],
            recv_sem=pair_recv.at[origin],
            device_id=(other, sub),
            device_id_type=MESH,
        )

    def rows_copy(i, origin):
        return pltpu.make_async_remote_copy(
            src_ref=mine,
            dst_ref=blocks.at[origin],
            send_sem=rows_send.at[i],
            recv_sem=rows_recv.at[origin],
            device_id=(strip, lax.rem(sub + i, subs)),
            device_id_type=MESH,
        )

    def loop(first, last, body):
        def step(i, carry):
            body(i)
            return carry

        lax.fori_loop(first, last, step, 0)

    for side in range(2):
        shift(side, 0).start()
        mask_copy(side).start()
    loop(1, strips, lambda i: ids_copy(i, strip).start())
    for j in range(1, ZP):
        for side in range(2):
            shift(side, j).start()

    ids_all[strip] = ids_out[...]
    loop(1, strips, lambda i: ids_copy(i, lax.rem(strip + strips - i, strips)).wait_recv())
    to_smem = pltpu.make_async_copy(ids_all, ids_smem, ids_sem)
    to_smem.start()
    loads[1].wait()
    to_smem.wait()

    def stage(other):
        count = jnp.int32(0)
        picks = [jnp.int32(0)] * CAP
        for r in range(wants):
            place = ids_smem[other, 0, r] - strip * owned
            here = (place >= 0) & (place < owned)
            for j in range(CAP):
                picks[j] = jnp.where(here & (count == j), place, picks[j])
            count = count + jnp.where(here, 1, 0)
        for j in range(CAP):
            staging[other, j] = pairs[picks[j]]

    loop(0, strips, stage)
    got[strip] = staging[strip]

    loads[0].wait()
    for side in range(2):
        mask_copy(side).wait_recv()

    def slot_of(i):
        place = nbr_ids_ref[i // nbrs, i % nbrs] - (strip - 1) * tri
        return jnp.clip(jnp.where(place >= 2 * tri, place - tri, place), 0, 2 * tri - 1)

    zr = lax.broadcasted_iota(jnp.int32, (width, width), 0)
    zc = lax.broadcasted_iota(jnp.int32, (width, width), 1)
    for t in range(tri):
        w = jnp.zeros((width, width), F32)
        factor = jnp.zeros((1, width), F32)
        for n in range(nbrs):
            i = t * nbrs + n
            mask = masks_in[slot_of(i)]
            raw = s_raw[t, n]
            s_mask[i] = (raw.astype(F32) * mask[0:1]).astype(BF16)
            choose = (zc // share == n) & (zr == lax.rem(zc, share) + sub * share)
            w = w + jnp.dot(raw, jnp.where(choose, 1.0, 0.0).astype(BF16), preferred_element_type=F32)
            factor = jnp.where(lane // share == n, mask[1:2] * fock_ref[t, n], factor)
        w_all[t] = (w * factor).astype(BF16)

    def project(j):
        for side in range(2):
            shift(side, j).wait_recv()

        def pair(i):
            slot = slot_of(i)
            s = s_mask[i]
            halves = []
            for q in range(zs // 2):
                m = held[j][slot, pl.ds(2 * q, 2)]
                both = jnp.concatenate([m[0], m[1]], axis=1)
                h = jnp.dot(s, both, preferred_element_type=F32).astype(BF16)
                halves += [h[:, :width], h[:, width:]]
            full = jnp.concatenate(halves, axis=0)
            p = lax.dot_general(full, s, (((1,), (1,)), ((), ())), preferred_element_type=F32)
            pbuf[pl.ds((i * share + j * zs) * width, zs * width), :] = p

        loop(0, tri * nbrs, pair)

    for j in range(ZP):
        project(j)

    def ring(step, e):
        way = lax.rem(e, 2)
        t = e // (2 * AP)
        p = lax.rem(e // 2, AP)
        sign = 1 - 2 * way
        chunk = lax.rem(sub - sign * (1 + step) + 2 * subs, subs)
        a0 = way * (width // 2) + p * rows_p
        return chunk, t, a0, pltpu.make_async_remote_copy(
            src_ref=part.at[t, chunk, pl.ds(a0, rows_p)],
            dst_ref=recv.at[step, t, pl.ds(a0, rows_p)],
            send_sem=ring_send.at[step, e],
            recv_sem=ring_recv.at[step, e],
            device_id=(strip, lax.rem(sub + sign + subs, subs)),
            device_id_type=MESH,
        )

    each = 2 * AP
    pieces = tri * each

    def couple(e):
        chunk, t, a0, copy = ring(0, e)

        def some(i):
            a = a0 + 4 * i
            w = w_all[t][:, :k]
            for v in range(2):
                both = jnp.concatenate(
                    [
                        pbuf[pl.ds(t * k * width + a + 2 * v + u, k, stride=width), :].astype(BF16)
                        for u in range(2)
                    ],
                    axis=1,
                )
                o = jnp.dot(w, both, preferred_element_type=F32).astype(BF16)
                for u in range(2):
                    for d in range(subs):
                        part[t, d, a + 2 * v + u] = o[d * share:(d + 1) * share, u * width:(u + 1) * width]

        loop(0, rows_p // 4, some)
        copy.start()

    loop(0, each, couple)
    loop(1, strips, lambda i: pair_copy(i, strip).start())
    loop(each, pieces, couple)

    def onward(step, e):
        _, _, _, before = ring(step - 1, e)
        chunk, t, a0, copy = ring(step, e)
        before.wait_recv()
        rows = pl.ds(a0, rows_p)
        total = part[t, chunk, rows].astype(F32) + recv[step - 1, t, rows].astype(F32)
        part[t, chunk, rows] = total.astype(BF16)
        copy.start()

    for step in range(1, subs - 1):
        loop(0, pieces, functools.partial(onward, step))
        if step == 1:
            loop(1, strips, lambda i: pair_copy(i, lax.rem(strip + strips - i, strips)).wait_recv())
            for r in range(wants):
                owner = pair_ids_ref[r // 3, r % 3] // owned
                rank = jnp.int32(0)
                for before_r in range(r):
                    rank = rank + jnp.where(pair_ids_ref[before_r // 3, before_r % 3] // owned == owner, 1, 0)
                mine[r] = got[owner, jnp.minimum(rank, CAP - 1)]
            for i in range(1, subs):
                rows_copy(i, sub).start()
            blocks[sub] = mine[...]

    loads[2].wait()
    loads[3].wait()
    loads[4].wait()
    for i in range(1, subs):
        rows_copy(i, lax.rem(sub + subs - i, subs)).wait_recv()
    for t in range(tri):
        tno = []
        for r in range(3):
            block = jnp.concatenate([blocks[y, t * 3 + r] for y in range(subs)], axis=0)
            o = over[t, r]
            left = jnp.dot(o, block, preferred_element_type=F32).astype(BF16)
            tno.append(
                lax.dot_general(left, o, (((1,), (1,)), ((), ())), preferred_element_type=F32).astype(BF16)
            )
        tno = jnp.concatenate(tno, axis=1)
        size = size_ref[t]
        live_ab = (zr < size) & (zc < size)
        energy_b = jnp.broadcast_to(energy_rows_ref[t:t + 1], (width, width))
        lmo_total = lmo_ref[triples_ref[t, 0]] + lmo_ref[triples_ref[t, 1]] + lmo_ref[triples_ref[t, 2]]
        den_ab = energy_b.T + energy_b - lmo_total

        def direct(v, t=t, tno=tno, size=size, live_ab=live_ab, den_ab=den_ab):
            both = jnp.concatenate(
                [
                    jnp.concatenate([ints[t, r, 2 * v + u] for r in range(3)], axis=0)
                    for u in range(2)
                ],
                axis=1,
            )
            x = jnp.dot(tno, both, preferred_element_type=F32)
            for u in range(2):
                c = 2 * v + u
                xu = x[:, u * width:(u + 1) * width]
                wsum = xu + xu.T
                live = live_ab & (sub * share + c < size)
                current = amp[t, c].astype(F32)
                den = den_ab + energy_ref[t, sub * share + c]
                scale = 0.7 / den
                base = current - scale * (wsum + den * current)
                at = (t * share + c) * width
                pbuf[pl.ds(flat + at, width), :] = jnp.where(live, base, 0.0)
                pbuf[pl.ds(2 * flat + at, width), :] = jnp.where(live, scale, 0.0)

        loop(0, share // 2, direct)

    def finish(e):
        _, t, a0, before = ring(subs - 2, e)
        before.wait_recv()

        def some(i):
            for u in range(4):
                a = a0 + 4 * i + u
                total = part[t, sub, a].astype(F32) + recv[subs - 2, t, a].astype(F32)
                pbuf[pl.ds(t * share * width + a, share, stride=width), :] = total

        loop(0, rows_p // 4, some)

    def update(t, c):
        at = (t * share + c) * width
        out_ref[t, c] = (
            pbuf[pl.ds(flat + at, width), :]
            + pbuf[pl.ds(2 * flat + at, width), :] * pbuf[pl.ds(at, width), :]
        ).astype(BF16)

    for t in range(tri):
        loop(t * each, (t + 1) * each, finish)
        loop(0, share, functools.partial(update, t))

    for side in range(2):
        mask_copy(side).wait_send()
        for j in range(ZP):
            shift(side, j).wait_send()
    loop(1, strips, lambda i: ids_copy(i, strip).wait_send())
    loop(1, strips, lambda i: pair_copy(i, strip).wait_send())
    for i in range(1, subs):
        rows_copy(i, sub).wait_send()
    for step in range(subs - 1):
        loop(0, pieces, lambda e: ring(step, e)[3].wait_send())


def local(
    amplitudes,
    tno_size,
    pair_amps,
    integrals,
    pair_intersection,
    nbr_intersection,
    tno_energy,
    lmo_energy,
    triples,
    pair_ids,
    nbr_ids,
    nbr_fock,
):
    tri, share, width, _ = amplitudes.shape
    nbrs = nbr_ids.shape[1]
    owned = pair_amps.shape[0]
    strips = lax.axis_size("strip")
    subs = lax.axis_size("sub")
    pieces = tri * 2 * AP
    smem = pl.BlockSpec(memory_space=pltpu.SMEM)
    vmem = pl.BlockSpec(memory_space=pltpu.VMEM)
    far = pl.BlockSpec(memory_space=pl.ANY)
    dma = pltpu.SemaphoreType.DMA
    return pl.pallas_call(
        functools.partial(kernel, strips, subs, tri, nbrs, share, width, owned),
        out_shape=jax.ShapeDtypeStruct(amplitudes.shape, BF16),
        in_specs=[smem] * 7 + [vmem] + [far] * 5,
        out_specs=vmem,
        scratch_shapes=[
            *[pltpu.VMEM((2 * tri, share // ZP, width, width), BF16) for _ in range(ZP)],
            pltpu.VMEM((tri * nbrs * share * width, width), F32),
            pltpu.VMEM((tri, subs, width, share, width), BF16),
            pltpu.VMEM((subs - 1, tri, width, share, width), BF16),
            pltpu.VMEM(integrals.shape, BF16),
            pltpu.VMEM(amplitudes.shape, BF16),
            pltpu.VMEM(pair_amps.shape, BF16),
            pltpu.VMEM(pair_intersection.shape, BF16),
            pltpu.VMEM(nbr_intersection.shape, BF16),
            pltpu.VMEM((tri * nbrs, width, width), BF16),
            pltpu.VMEM((tri, width, width), BF16),
            pltpu.VMEM((tri, 8, width), F32),
            pltpu.VMEM((2 * tri, 8, width), F32),
            pltpu.VMEM((1, width), jnp.int32),
            pltpu.VMEM((strips, 1, width), jnp.int32),
            pltpu.SMEM((strips, 1, width), jnp.int32),
            pltpu.VMEM((strips, CAP, share, width), BF16),
            pltpu.VMEM((strips, CAP, share, width), BF16),
            pltpu.VMEM((tri * 3, share, width), BF16),
            pltpu.VMEM((subs, tri * 3, share, width), BF16),
            dma((5,)),
            dma((2,)),
            dma((2,)),
            dma,
            dma((strips,)),
            dma((strips,)),
            dma((2, ZP)),
            dma((2, ZP)),
            dma((strips,)),
            dma((strips,)),
            dma((subs,)),
            dma((subs,)),
            dma((subs - 1, pieces)),
            dma((subs - 1, pieces)),
        ],
        compiler_params=pltpu.CompilerParams(
            collective_id=0, has_side_effects=True, vmem_limit_bytes=60 * 1024 * 1024
        ),
    )(
        tno_size, pair_ids, nbr_ids, nbr_fock, triples, lmo_energy, tno_energy,
        tno_energy, amplitudes, pair_amps, integrals, pair_intersection, nbr_intersection,
    )


def solution(mesh):
    in_specs = (
        P("strip", "sub", None, None),
        P("strip"),
        P("strip", "sub", None),
        P("strip", None, "sub", None, None),
        P("strip", None, None, None),
        P("strip", None, None, None),
        P("strip", None),
        P(),
        P("strip", None),
        P("strip", None),
        P("strip", None),
        P("strip", None),
    )
    out_specs = P("strip", "sub", None, None)
    return jax.shard_map(local, mesh=mesh, in_specs=in_specs, out_specs=out_specs, check_vma=False)
```

```python
import functools

import jax
import jax.numpy as jnp
from jax import lax
from jax.experimental import pallas as pl
from jax.experimental.pallas import tpu as pltpu
from jax.sharding import PartitionSpec as P

MESH = pl.DeviceIdType.MESH
F32 = jnp.float32
BF16 = jnp.bfloat16
ZP = 4
AP = 4
CAP = 2
Z = 8
CORES = 2
STRIDE_PAD = 8


def kernel(
    strips, subs, tri, nbrs, share, width, owned,
    size_ref, pair_ids_ref, nbr_ids_ref, fock_ref, triples_ref, lmo_ref, energy_ref,
    energy_rows_ref, amp_ref, pairs_ref, ints_ref, over_ref, inter_ref,
    out_ref,
    held0, held1, held2, held3, pbuf, part, recv, ints, amp, pairs, over, s_raw, s_mask, w_all,
    masks_out, masks_in, ids_out, ids_all, ids_smem, staging, got, staging_z, got_z, mine, blocks,
    local_sem, mask_send, mask_recv, ids_sem, ids_send, ids_recv, shift_send, shift_recv,
    ids_send_z, ids_recv_z, pair_send, pair_recv, pair_send_z, pair_recv_z, rows_send, rows_recv, ring_send, ring_recv,
):
    strip = lax.axis_index("strip")
    sub = lax.axis_index("sub")
    up = lax.rem(strip + 1, strips)
    down = lax.rem(strip + strips - 1, strips)
    planes = strips // Z
    z = lax.rem(lax.div(strip, CORES), Z)
    plane = lax.div(strip, Z * CORES) * CORES + lax.rem(strip, CORES)
    far_side = jnp.where(lax.rem(strip, CORES) == 0, down, up)

    def strip_at(plane, z):
        return (lax.div(plane, CORES) * Z + z) * CORES + lax.rem(plane, CORES)

    zs = share // ZP
    stride = width + STRIDE_PAD
    rows_p = width // 2 // AP
    k = nbrs * share
    wants = tri * 3
    flat = tri * share * width
    base_at = tri * share * stride

    held = (held0, held1, held2, held3)
    loads = [
        pltpu.make_async_copy(src, dst, local_sem.at[i])
        for i, (src, dst) in enumerate(
            [(inter_ref, s_raw), (pairs_ref, pairs), (over_ref, over), (amp_ref, amp), (ints_ref, ints)]
        )
    ]
    for copy in loads:
        copy.start()

    barrier = pltpu.get_barrier_semaphore()

    greeted = [(strip_at(lax.rem(plane + i, planes), z), sub) for i in range(1, planes)]
    greeted += [(strip_at(plane, lax.rem(z + i, Z)), sub) for i in range(1, Z)]
    greeted += [(strip, lax.rem(sub + i, subs)) for i in range(1, subs)]
    greeted += [(far_side, sub)]
    for device in greeted:
        pl.semaphore_signal(barrier, inc=1, device_id=device, device_id_type=MESH)

    lane = lax.broadcasted_iota(jnp.int32, (1, width), 1)
    for t in range(tri):
        size = size_ref[t]
        masks_out[t, 0:1] = jnp.where(lane < size, 1.0, 0.0).astype(F32)
        masks_out[t, 1:2] = jnp.where(lax.rem(lane, share) + sub * share < size, 1.0, 0.0).astype(F32)
        masks_out[t, 2:8] = jnp.zeros((6, width), F32)
    row = jnp.zeros((1, width), jnp.int32)
    for r in range(wants):
        row = jnp.where(lane == r, pair_ids_ref[r // 3, r % 3], row)
    ids_out[...] = row
    pl.semaphore_wait(barrier, len(greeted))

    def mask_copy(side):
        return pltpu.make_async_remote_copy(
            src_ref=masks_out,
            dst_ref=masks_in.at[pl.ds(side * tri, tri)],
            send_sem=mask_send.at[side],
            recv_sem=mask_recv.at[side],
            device_id=((up if side == 0 else down), sub),
            device_id_type=MESH,
        )

    def shift(side, j):
        return pltpu.make_async_remote_copy(
            src_ref=amp_ref.at[:, pl.ds(j * zs, zs)],
            dst_ref=held[j].at[pl.ds(side * tri, tri)],
            send_sem=shift_send.at[side, j],
            recv_sem=shift_recv.at[side, j],
            device_id=((up if side == 0 else down), sub),
            device_id_type=MESH,
        )

    def ids_copy(i, origin):
        return pltpu.make_async_remote_copy(
            src_ref=ids_out,
            dst_ref=ids_all.at[z * planes + origin],
            send_sem=ids_send.at[i],
            recv_sem=ids_recv.at[origin],
            device_id=(strip_at(lax.rem(plane + i, planes), z), sub),
            device_id_type=MESH,
        )

    def ids_copy_z(i, origin):
        return pltpu.make_async_remote_copy(
            src_ref=ids_all.at[pl.ds(z * planes, planes)],
            dst_ref=ids_all.at[pl.ds(origin * planes, planes)],
            send_sem=ids_send_z.at[i],
            recv_sem=ids_recv_z.at[origin],
            device_id=(strip_at(plane, lax.rem(z + i, Z)), sub),
            device_id_type=MESH,
        )

    def pair_copy(i, origin):
        other = lax.rem(plane + i, planes)
        return pltpu.make_async_remote_copy(
            src_ref=staging.at[other],
            dst_ref=got.at[origin],
            send_sem=pair_send.at[i],
            recv_sem=pair_recv.at[origin],
            device_id=(strip_at(other, z), sub),
            device_id_type=MESH,
        )

    def pair_copy_z(i, origin):
        other = lax.rem(z + i, Z)
        return pltpu.make_async_remote_copy(
            src_ref=staging_z.at[other],
            dst_ref=got_z.at[origin],
            send_sem=pair_send_z.at[i],
            recv_sem=pair_recv_z.at[origin],
            device_id=(strip_at(plane, other), sub),
            device_id_type=MESH,
        )

    def rows_copy(i, origin):
        return pltpu.make_async_remote_copy(
            src_ref=mine,
            dst_ref=blocks.at[origin],
            send_sem=rows_send.at[i],
            recv_sem=rows_recv.at[origin],
            device_id=(strip, lax.rem(sub + i, subs)),
            device_id_type=MESH,
        )

    def loop(first, last, body, unroll=1):
        def step(i, carry):
            body(i)
            return carry

        lax.fori_loop(first, last, step, 0, unroll=unroll)

    for side in range(2):
        shift(side, 0).start()
        mask_copy(side).start()
    for i in range(1, planes):
        ids_copy(i, plane).start()
    for j in range(1, ZP):
        for side in range(2):
            shift(side, j).start()

    ids_all[z * planes + plane] = ids_out[...]
    for i in range(1, planes):
        ids_copy(i, lax.rem(plane + planes - i, planes)).wait_recv()
    for i in range(1, Z):
        ids_copy_z(i, z).start()
    loads[1].wait()
    for i in range(1, Z):
        ids_copy_z(i, lax.rem(z + Z - i, Z)).wait_recv()
    to_smem = pltpu.make_async_copy(ids_all, ids_smem, ids_sem)
    to_smem.start()
    to_smem.wait()

    def stage(m):
        count = jnp.int32(0)
        picks = [jnp.int32(0)] * CAP
        for r in range(wants):
            place = ids_smem[m, 0, r] - strip * owned
            here = (place >= 0) & (place < owned)
            for j in range(CAP):
                picks[j] = jnp.where(here & (count == j), place, picks[j])
            count = count + jnp.where(here, 1, 0)
        for j in range(CAP):
            staging[lax.rem(m, planes), lax.div(m, planes), j] = pairs[picks[j]]

    loop(0, strips, stage)
    for i in range(1, planes):
        pair_copy(i, plane).start()
    got[plane] = staging[plane]

    loads[0].wait()
    for side in range(2):
        mask_copy(side).wait_recv()

    def slot_of(i):
        place = nbr_ids_ref[i // nbrs, i % nbrs] - (strip - 1) * tri
        return jnp.clip(jnp.where(place >= 2 * tri, place - tri, place), 0, 2 * tri - 1)

    zr = lax.broadcasted_iota(jnp.int32, (width, width), 0)
    zc = lax.broadcasted_iota(jnp.int32, (width, width), 1)
    for t in range(tri):
        w = jnp.zeros((width, width), F32)
        factor = jnp.zeros((1, width), F32)
        for n in range(nbrs):
            i = t * nbrs + n
            mask = masks_in[slot_of(i)]
            raw = s_raw[t, n]
            s_mask[i] = (raw.astype(F32) * mask[0:1]).astype(BF16)
            choose = (zc // share == n) & (zr == lax.rem(zc, share) + sub * share)
            w = w + jnp.dot(raw, jnp.where(choose, 1.0, 0.0).astype(BF16), preferred_element_type=F32)
            factor = jnp.where(lane // share == n, mask[1:2] * fock_ref[t, n], factor)
        w_all[t] = (w * factor).astype(BF16)

    def project(j):
        for side in range(2):
            shift(side, j).wait_recv()

        def pair(i):
            slot = slot_of(i)
            s = s_mask[i]
            halves = []
            for q in range(zs // 2):
                m = held[j][slot, pl.ds(2 * q, 2)]
                both = jnp.concatenate([m[0], m[1]], axis=1)
                h = jnp.dot(s, both, preferred_element_type=F32).astype(BF16)
                halves += [h[:, :width], h[:, width:]]
            full = jnp.concatenate(halves, axis=0)
            p = lax.dot_general(full, s, (((1,), (1,)), ((), ())), preferred_element_type=F32)
            for q in range(zs):
                pbuf[pl.ds((i * share + j * zs + q) * stride, width), :] = p[q * width:(q + 1) * width]

        loop(0, tri * nbrs, pair, unroll=tri * nbrs)

    for j in range(ZP):
        project(j)

    def ring(step, e):
        way = lax.rem(e, 2)
        t = e // (2 * AP)
        p = lax.rem(e // 2, AP)
        sign = 1 - 2 * way
        chunk = lax.rem(sub - sign * (1 + step) + 2 * subs, subs)
        a0 = way * (width // 2) + p * rows_p
        return chunk, t, a0, pltpu.make_async_remote_copy(
            src_ref=part.at[t, chunk, pl.ds(a0, rows_p)],
            dst_ref=recv.at[step, t, pl.ds(a0, rows_p)],
            send_sem=ring_send.at[step, e],
            recv_sem=ring_recv.at[step, e],
            device_id=(strip, lax.rem(sub + sign + subs, subs)),
            device_id_type=MESH,
        )

    each = 2 * AP
    pieces = tri * each

    def couple(e):
        chunk, t, a0, copy = ring(0, e)

        def some(i):
            a = a0 + 4 * i
            w = w_all[t][:, :k]
            for v in range(2):
                both = jnp.concatenate(
                    [
                        pbuf[pl.ds(t * k * stride + a + 2 * v + u, k, stride=stride), :].astype(BF16)
                        for u in range(2)
                    ],
                    axis=1,
                )
                o = jnp.dot(w, both, preferred_element_type=F32).astype(BF16)
                for u in range(2):
                    for d in range(subs):
                        part[t, d, a + 2 * v + u] = o[d * share:(d + 1) * share, u * width:(u + 1) * width]

        loop(0, rows_p // 4, some, unroll=rows_p // 4)
        copy.start()

    loop(0, each, couple)
    for i in range(1, planes):
        pair_copy(i, lax.rem(plane + planes - i, planes)).wait_recv()

    def merge(other):
        owners = [lax.div(ids_smem[other * planes + plane, 0, r], owned) for r in range(wants)]
        for r in range(wants):
            rank = jnp.int32(0)
            for q in range(r):
                rank = rank + jnp.where(owners[q] == owners[r], 1, 0)
            source = lax.div(owners[r], Z * CORES) * CORES + lax.rem(owners[r], CORES)
            staging_z[other, r] = got[source, other, jnp.minimum(rank, CAP - 1)]

    loop(0, Z, merge)
    for i in range(1, Z):
        pair_copy_z(i, z).start()
    got_z[z] = staging_z[z]
    loop(each, pieces, couple)

    def onward(step, e):
        _, _, _, before = ring(step - 1, e)
        chunk, t, a0, copy = ring(step, e)
        before.wait_recv()
        rows = pl.ds(a0, rows_p)
        total = part[t, chunk, rows].astype(F32) + recv[step - 1, t, rows].astype(F32)
        part[t, chunk, rows] = total.astype(BF16)
        copy.start()

    for step in range(1, subs - 1):
        loop(0, pieces, functools.partial(onward, step))
        if step == 1:
            for i in range(1, Z):
                pair_copy_z(i, lax.rem(z + Z - i, Z)).wait_recv()
            for r in range(wants):
                owner = lax.div(pair_ids_ref[r // 3, r % 3], owned)
                mine[r] = got_z[lax.rem(lax.div(owner, CORES), Z), r]
            for i in range(1, subs):
                rows_copy(i, sub).start()
            blocks[sub] = mine[...]

    loads[2].wait()
    loads[3].wait()
    loads[4].wait()
    for i in range(1, subs):
        rows_copy(i, lax.rem(sub + subs - i, subs)).wait_recv()
    for t in range(tri):
        tno = []
        for r in range(3):
            block = jnp.concatenate([blocks[y, t * 3 + r] for y in range(subs)], axis=0)
            o = over[t, r]
            left = jnp.dot(o, block, preferred_element_type=F32).astype(BF16)
            tno.append(
                lax.dot_general(left, o, (((1,), (1,)), ((), ())), preferred_element_type=F32).astype(BF16)
            )
        tno = jnp.concatenate(tno, axis=1)
        size = size_ref[t]
        live_ab = (zr < size) & (zc < size)
        energy_b = jnp.broadcast_to(energy_rows_ref[t:t + 1], (width, width))
        lmo_total = lmo_ref[triples_ref[t, 0]] + lmo_ref[triples_ref[t, 1]] + lmo_ref[triples_ref[t, 2]]
        den_ab = energy_b.T + energy_b - lmo_total

        def direct(v, t=t, tno=tno, size=size, live_ab=live_ab, den_ab=den_ab):
            both = jnp.concatenate(
                [
                    jnp.concatenate([ints[t, r, 2 * v + u] for r in range(3)], axis=0)
                    for u in range(2)
                ],
                axis=1,
            )
            x = jnp.dot(tno, both, preferred_element_type=F32)
            for u in range(2):
                c = 2 * v + u
                xu = x[:, u * width:(u + 1) * width]
                wsum = xu + xu.T
                live = live_ab & (sub * share + c < size)
                current = amp[t, c].astype(F32)
                den = den_ab + energy_ref[t, sub * share + c]
                scale = 0.7 / den
                base = current - scale * (wsum + den * current)
                at = base_at + (t * share + c) * width
                pbuf[pl.ds(at, width), :] = jnp.where(live, base, 0.0)
                pbuf[pl.ds(flat + at, width), :] = jnp.where(live, scale, 0.0)

        loop(0, share // 2, direct, unroll=4)

    def finish(e):
        _, t, a0, before = ring(subs - 2, e)
        before.wait_recv()

        def some(i):
            for u in range(4):
                a = a0 + 4 * i + u
                total = part[t, sub, a].astype(F32) + recv[subs - 2, t, a].astype(F32)
                pbuf[pl.ds(t * share * stride + a, share, stride=stride), :] = total

        loop(0, rows_p // 4, some, unroll=rows_p // 4)

    def update(t, c):
        at = base_at + (t * share + c) * width
        out_ref[t, c] = (
            pbuf[pl.ds(at, width), :]
            + pbuf[pl.ds(flat + at, width), :] * pbuf[pl.ds((t * share + c) * stride, width), :]
        ).astype(BF16)

    for side in range(2):
        mask_copy(side).wait_send()
        for j in range(ZP):
            shift(side, j).wait_send()
    for i in range(1, planes):
        ids_copy(i, plane).wait_send()
        pair_copy(i, plane).wait_send()
    for i in range(1, Z):
        ids_copy_z(i, z).wait_send()
        pair_copy_z(i, z).wait_send()
    for i in range(1, subs):
        rows_copy(i, sub).wait_send()
    for step in range(subs - 2):
        loop(0, pieces, lambda e: ring(step, e)[3].wait_send())

    for t in range(tri):
        loop(t * each, (t + 1) * each, finish)
        loop(0, share, functools.partial(update, t), unroll=2)
    loop(0, pieces, lambda e: ring(subs - 2, e)[3].wait_send())


def local(
    amplitudes,
    tno_size,
    pair_amps,
    integrals,
    pair_intersection,
    nbr_intersection,
    tno_energy,
    lmo_energy,
    triples,
    pair_ids,
    nbr_ids,
    nbr_fock,
):
    tri, share, width, _ = amplitudes.shape
    nbrs = nbr_ids.shape[1]
    owned = pair_amps.shape[0]
    strips = lax.axis_size("strip")
    subs = lax.axis_size("sub")
    pieces = tri * 2 * AP
    smem = pl.BlockSpec(memory_space=pltpu.SMEM)
    vmem = pl.BlockSpec(memory_space=pltpu.VMEM)
    far = pl.BlockSpec(memory_space=pl.ANY)
    dma = pltpu.SemaphoreType.DMA
    return pl.pallas_call(
        functools.partial(kernel, strips, subs, tri, nbrs, share, width, owned),
        out_shape=jax.ShapeDtypeStruct(amplitudes.shape, BF16),
        in_specs=[smem] * 7 + [vmem] + [far] * 5,
        out_specs=vmem,
        scratch_shapes=[
            *[pltpu.VMEM((2 * tri, share // ZP, width, width), BF16) for _ in range(ZP)],
            pltpu.VMEM((tri * nbrs * share * (width + STRIDE_PAD), width), F32),
            pltpu.VMEM((tri, subs, width, share, width), BF16),
            pltpu.VMEM((subs - 1, tri, width, share, width), BF16),
            pltpu.VMEM(integrals.shape, BF16),
            pltpu.VMEM(amplitudes.shape, BF16),
            pltpu.VMEM(pair_amps.shape, BF16),
            pltpu.VMEM(pair_intersection.shape, BF16),
            pltpu.VMEM(nbr_intersection.shape, BF16),
            pltpu.VMEM((tri * nbrs, width, width), BF16),
            pltpu.VMEM((tri, width, width), BF16),
            pltpu.VMEM((tri, 8, width), F32),
            pltpu.VMEM((2 * tri, 8, width), F32),
            pltpu.VMEM((1, width), jnp.int32),
            pltpu.VMEM((strips, 1, width), jnp.int32),
            pltpu.SMEM((strips, 1, width), jnp.int32),
            pltpu.VMEM((strips // Z, Z, CAP, share, width), BF16),
            pltpu.VMEM((strips // Z, Z, CAP, share, width), BF16),
            pltpu.VMEM((Z, tri * 3, share, width), BF16),
            pltpu.VMEM((Z, tri * 3, share, width), BF16),
            pltpu.VMEM((tri * 3, share, width), BF16),
            pltpu.VMEM((subs, tri * 3, share, width), BF16),
            dma((5,)),
            dma((2,)),
            dma((2,)),
            dma,
            dma((strips // Z,)),
            dma((strips // Z,)),
            dma((2, ZP)),
            dma((2, ZP)),
            dma((Z,)),
            dma((Z,)),
            dma((strips // Z,)),
            dma((strips // Z,)),
            dma((Z,)),
            dma((Z,)),
            dma((subs,)),
            dma((subs,)),
            dma((subs - 1, pieces)),
            dma((subs - 1, pieces)),
        ],
        compiler_params=pltpu.CompilerParams(
            collective_id=0, has_side_effects=True, vmem_limit_bytes=60 * 1024 * 1024
        ),
    )(
        tno_size, pair_ids, nbr_ids, nbr_fock, triples, lmo_energy, tno_energy,
        tno_energy, amplitudes, pair_amps, integrals, pair_intersection, nbr_intersection,
    )


def solution(mesh):
    in_specs = (
        P("strip", "sub", None, None),
        P("strip"),
        P("strip", "sub", None),
        P("strip", None, "sub", None, None),
        P("strip", None, None, None),
        P("strip", None, None, None),
        P("strip", None),
        P(),
        P("strip", None),
        P("strip", None),
        P("strip", None),
        P("strip", None),
    )
    out_specs = P("strip", "sub", None, None)
    return jax.shard_map(local, mesh=mesh, in_specs=in_specs, out_specs=out_specs, check_vma=False)
```

```python
import functools

import jax
import jax.numpy as jnp
from jax import lax
from jax.experimental import pallas as pl
from jax.experimental.pallas import tpu as pltpu
from jax.sharding import PartitionSpec as P

MESH = pl.DeviceIdType.MESH
F32 = jnp.float32
BF16 = jnp.bfloat16
ZP = 4
AP = 4
CAP = 2
Z = 8
CORES = 2
STRIDE_PAD = 8


def kernel(
    strips, subs, tri, nbrs, share, width, owned,
    size_ref, pair_ids_ref, nbr_ids_ref, fock_ref, triples_ref, lmo_ref, energy_ref,
    energy_rows_ref, amp_ref, pairs_ref, ints_ref, over_ref, inter_ref,
    out_ref,
    held0, held1, held2, held3, pbuf, part, recv, ints, amp, pairs, over, s_raw, s_mask, w_all,
    masks_out, masks_in, ids_out, ids_all, ids_smem, staging, got, staging_z, got_z, mine, blocks,
    local_sem, mask_send, mask_recv, ids_sem, ids_send, ids_recv, shift_send, shift_recv,
    ids_send_z, ids_recv_z, pair_send, pair_recv, pair_send_z, pair_recv_z, rows_send, rows_recv, ring_send, ring_recv,
):
    strip = lax.axis_index("strip")
    sub = lax.axis_index("sub")
    up = lax.rem(strip + 1, strips)
    down = lax.rem(strip + strips - 1, strips)
    planes = strips // Z
    z = lax.rem(lax.div(strip, CORES), Z)
    plane = lax.div(strip, Z * CORES) * CORES + lax.rem(strip, CORES)
    far_side = jnp.where(lax.rem(strip, CORES) == 0, down, up)

    def strip_at(plane, z):
        return (lax.div(plane, CORES) * Z + z) * CORES + lax.rem(plane, CORES)

    zs = share // ZP
    stride = width + STRIDE_PAD
    rows_p = width // 2 // AP
    k = nbrs * share
    wants = tri * 3
    flat = tri * share * width
    base_at = tri * share * stride

    held = (held0, held1, held2, held3)
    loads = [
        pltpu.make_async_copy(src, dst, local_sem.at[i])
        for i, (src, dst) in enumerate(
            [(inter_ref, s_raw), (pairs_ref, pairs), (over_ref, over), (amp_ref, amp), (ints_ref, ints)]
        )
    ]
    for copy in loads:
        copy.start()

    barrier = pltpu.get_barrier_semaphore()

    greeted = [(strip_at(lax.rem(plane + i, planes), z), sub) for i in range(1, planes)]
    greeted += [(strip_at(plane, lax.rem(z + i, Z)), sub) for i in range(1, Z)]
    greeted += [(strip, lax.rem(sub + i, subs)) for i in range(1, subs)]
    greeted += [(far_side, sub)]
    for device in greeted:
        pl.semaphore_signal(barrier, inc=1, device_id=device, device_id_type=MESH)

    lane = lax.broadcasted_iota(jnp.int32, (1, width), 1)
    for t in range(tri):
        size = size_ref[t]
        masks_out[t, 0:1] = jnp.where(lane < size, 1.0, 0.0).astype(F32)
        masks_out[t, 1:2] = jnp.where(lax.rem(lane, share) + sub * share < size, 1.0, 0.0).astype(F32)
        masks_out[t, 2:8] = jnp.zeros((6, width), F32)
    row = jnp.zeros((1, width), jnp.int32)
    for r in range(wants):
        row = jnp.where(lane == r, pair_ids_ref[r // 3, r % 3], row)
    ids_out[...] = row
    pl.semaphore_wait(barrier, len(greeted))

    def mask_copy(side):
        return pltpu.make_async_remote_copy(
            src_ref=masks_out,
            dst_ref=masks_in.at[pl.ds(side * tri, tri)],
            send_sem=mask_send.at[side],
            recv_sem=mask_recv.at[side],
            device_id=((up if side == 0 else down), sub),
            device_id_type=MESH,
        )

    def shift(side, j):
        return pltpu.make_async_remote_copy(
            src_ref=amp_ref.at[:, pl.ds(j * zs, zs)],
            dst_ref=held[j].at[pl.ds(side * tri, tri)],
            send_sem=shift_send.at[side, j],
            recv_sem=shift_recv.at[side, j],
            device_id=((up if side == 0 else down), sub),
            device_id_type=MESH,
        )

    def ids_copy(i, origin):
        return pltpu.make_async_remote_copy(
            src_ref=ids_out,
            dst_ref=ids_all.at[z * planes + origin],
            send_sem=ids_send.at[i],
            recv_sem=ids_recv.at[origin],
            device_id=(strip_at(lax.rem(plane + i, planes), z), sub),
            device_id_type=MESH,
        )

    def ids_copy_z(i, origin):
        return pltpu.make_async_remote_copy(
            src_ref=ids_all.at[pl.ds(z * planes, planes)],
            dst_ref=ids_all.at[pl.ds(origin * planes, planes)],
            send_sem=ids_send_z.at[i],
            recv_sem=ids_recv_z.at[origin],
            device_id=(strip_at(plane, lax.rem(z + i, Z)), sub),
            device_id_type=MESH,
        )

    def pair_copy(i, origin):
        other = lax.rem(plane + i, planes)
        return pltpu.make_async_remote_copy(
            src_ref=staging.at[other],
            dst_ref=got.at[origin],
            send_sem=pair_send.at[i],
            recv_sem=pair_recv.at[origin],
            device_id=(strip_at(other, z), sub),
            device_id_type=MESH,
        )

    def pair_copy_z(i, origin):
        other = lax.rem(z + i, Z)
        return pltpu.make_async_remote_copy(
            src_ref=staging_z.at[other],
            dst_ref=got_z.at[origin],
            send_sem=pair_send_z.at[i],
            recv_sem=pair_recv_z.at[origin],
            device_id=(strip_at(plane, other), sub),
            device_id_type=MESH,
        )

    def rows_copy(i, origin):
        return pltpu.make_async_remote_copy(
            src_ref=mine,
            dst_ref=blocks.at[origin],
            send_sem=rows_send.at[i],
            recv_sem=rows_recv.at[origin],
            device_id=(strip, lax.rem(sub + i, subs)),
            device_id_type=MESH,
        )

    def loop(first, last, body, unroll=1):
        def step(i, carry):
            body(i)
            return carry

        lax.fori_loop(first, last, step, 0, unroll=unroll)

    for side in range(2):
        mask_copy(side).start()
    for i in range(1, planes):
        ids_copy(i, plane).start()
    for j in range(2):
        for side in range(2):
            shift(side, j).start()
    ids_all[z * planes + plane] = ids_out[...]

    loads[0].wait()
    for side in range(2):
        mask_copy(side).wait_recv()

    def slot_of(i):
        place = nbr_ids_ref[i // nbrs, i % nbrs] - (strip - 1) * tri
        return jnp.clip(jnp.where(place >= 2 * tri, place - tri, place), 0, 2 * tri - 1)

    zr = lax.broadcasted_iota(jnp.int32, (width, width), 0)
    zc = lax.broadcasted_iota(jnp.int32, (width, width), 1)
    for t in range(tri):
        w = jnp.zeros((width, width), F32)
        factor = jnp.zeros((1, width), F32)
        for n in range(nbrs):
            i = t * nbrs + n
            mask = masks_in[slot_of(i)]
            raw = s_raw[t, n]
            s_mask[i] = (raw.astype(F32) * mask[0:1]).astype(BF16)
            choose = (zc // share == n) & (zr == lax.rem(zc, share) + sub * share)
            w = w + jnp.dot(raw, jnp.where(choose, 1.0, 0.0).astype(BF16), preferred_element_type=F32)
            factor = jnp.where(lane // share == n, mask[1:2] * fock_ref[t, n], factor)
        w_all[t] = (w * factor).astype(BF16)

    def project(j):
        for side in range(2):
            shift(side, j).wait_recv()

        def pair(i):
            slot = slot_of(i)
            s = s_mask[i]
            halves = []
            for q in range(zs // 2):
                m = held[j][slot, pl.ds(2 * q, 2)]
                both = jnp.concatenate([m[0], m[1]], axis=1)
                h = jnp.dot(s, both, preferred_element_type=F32).astype(BF16)
                halves += [h[:, :width], h[:, width:]]
            full = jnp.concatenate(halves, axis=0)
            p = lax.dot_general(full, s, (((1,), (1,)), ((), ())), preferred_element_type=F32)
            for q in range(zs):
                pbuf[pl.ds((i * share + j * zs + q) * stride, width), :] = p[q * width:(q + 1) * width]

        loop(0, tri * nbrs, pair, unroll=tri * nbrs)

    for i in range(1, planes):
        ids_copy(i, lax.rem(plane + planes - i, planes)).wait_recv()
    for i in range(1, Z):
        ids_copy_z(i, z).start()
    for side in range(2):
        shift(side, 2).start()
    project(0)
    for side in range(2):
        shift(side, 3).start()

    loads[1].wait()
    for i in range(1, Z):
        ids_copy_z(i, lax.rem(z + Z - i, Z)).wait_recv()
    to_smem = pltpu.make_async_copy(ids_all, ids_smem, ids_sem)
    to_smem.start()
    to_smem.wait()

    def stage(m):
        count = jnp.int32(0)
        picks = [jnp.int32(0)] * CAP
        for r in range(wants):
            place = ids_smem[m, 0, r] - strip * owned
            here = (place >= 0) & (place < owned)
            for j in range(CAP):
                picks[j] = jnp.where(here & (count == j), place, picks[j])
            count = count + jnp.where(here, 1, 0)
        for j in range(CAP):
            staging[lax.rem(m, planes), lax.div(m, planes), j] = pairs[picks[j]]

    loop(0, strips, stage)
    for i in range(1, planes):
        pair_copy(i, plane).start()
    got[plane] = staging[plane]
    for j in range(1, ZP):
        project(j)

    def ring(step, e):
        way = lax.rem(e, 2)
        t = e // (2 * AP)
        p = lax.rem(e // 2, AP)
        sign = 1 - 2 * way
        chunk = lax.rem(sub - sign * (1 + step) + 2 * subs, subs)
        a0 = way * (width // 2) + p * rows_p
        return chunk, t, a0, pltpu.make_async_remote_copy(
            src_ref=part.at[t, chunk, pl.ds(a0, rows_p)],
            dst_ref=recv.at[step, t, pl.ds(a0, rows_p)],
            send_sem=ring_send.at[step, e],
            recv_sem=ring_recv.at[step, e],
            device_id=(strip, lax.rem(sub + sign + subs, subs)),
            device_id_type=MESH,
        )

    each = 2 * AP
    pieces = tri * each

    def couple(e):
        chunk, t, a0, copy = ring(0, e)

        def some(i):
            a = a0 + 4 * i
            w = w_all[t][:, :k]
            for v in range(2):
                both = jnp.concatenate(
                    [
                        pbuf[pl.ds(t * k * stride + a + 2 * v + u, k, stride=stride), :].astype(BF16)
                        for u in range(2)
                    ],
                    axis=1,
                )
                o = jnp.dot(w, both, preferred_element_type=F32).astype(BF16)
                for u in range(2):
                    for d in range(subs):
                        part[t, d, a + 2 * v + u] = o[d * share:(d + 1) * share, u * width:(u + 1) * width]

        loop(0, rows_p // 4, some, unroll=rows_p // 4)
        copy.start()

    loop(0, each, couple)
    for i in range(1, planes):
        pair_copy(i, lax.rem(plane + planes - i, planes)).wait_recv()

    def merge(other):
        owners = [lax.div(ids_smem[other * planes + plane, 0, r], owned) for r in range(wants)]
        for r in range(wants):
            rank = jnp.int32(0)
            for q in range(r):
                rank = rank + jnp.where(owners[q] == owners[r], 1, 0)
            source = lax.div(owners[r], Z * CORES) * CORES + lax.rem(owners[r], CORES)
            staging_z[other, r] = got[source, other, jnp.minimum(rank, CAP - 1)]

    loop(0, Z, merge)
    for i in range(1, Z):
        pair_copy_z(i, z).start()
    got_z[z] = staging_z[z]
    loop(each, pieces, couple)

    def onward(step, e):
        _, _, _, before = ring(step - 1, e)
        chunk, t, a0, copy = ring(step, e)
        before.wait_recv()
        rows = pl.ds(a0, rows_p)
        total = part[t, chunk, rows].astype(F32) + recv[step - 1, t, rows].astype(F32)
        part[t, chunk, rows] = total.astype(BF16)
        copy.start()

    for step in range(1, subs - 1):
        loop(0, pieces, functools.partial(onward, step))
        if step == 1:
            for i in range(1, Z):
                pair_copy_z(i, lax.rem(z + Z - i, Z)).wait_recv()
            for r in range(wants):
                owner = lax.div(pair_ids_ref[r // 3, r % 3], owned)
                mine[r] = got_z[lax.rem(lax.div(owner, CORES), Z), r]
            for i in range(1, subs):
                rows_copy(i, sub).start()
            blocks[sub] = mine[...]

    loads[2].wait()
    loads[3].wait()
    loads[4].wait()
    for i in range(1, subs):
        rows_copy(i, lax.rem(sub + subs - i, subs)).wait_recv()
    for t in range(tri):
        tno = []
        for r in range(3):
            block = jnp.concatenate([blocks[y, t * 3 + r] for y in range(subs)], axis=0)
            o = over[t, r]
            left = jnp.dot(o, block, preferred_element_type=F32).astype(BF16)
            tno.append(
                lax.dot_general(left, o, (((1,), (1,)), ((), ())), preferred_element_type=F32).astype(BF16)
            )
        tno = jnp.concatenate(tno, axis=1)
        size = size_ref[t]
        live_ab = (zr < size) & (zc < size)
        energy_b = jnp.broadcast_to(energy_rows_ref[t:t + 1], (width, width))
        lmo_total = lmo_ref[triples_ref[t, 0]] + lmo_ref[triples_ref[t, 1]] + lmo_ref[triples_ref[t, 2]]
        den_ab = energy_b.T + energy_b - lmo_total

        def direct(v, t=t, tno=tno, size=size, live_ab=live_ab, den_ab=den_ab):
            both = jnp.concatenate(
                [
                    jnp.concatenate([ints[t, r, 2 * v + u] for r in range(3)], axis=0)
                    for u in range(2)
                ],
                axis=1,
            )
            x = jnp.dot(tno, both, preferred_element_type=F32)
            for u in range(2):
                c = 2 * v + u
                xu = x[:, u * width:(u + 1) * width]
                wsum = xu + xu.T
                live = live_ab & (sub * share + c < size)
                current = amp[t, c].astype(F32)
                den = den_ab + energy_ref[t, sub * share + c]
                scale = 0.7 / den
                base = current - scale * (wsum + den * current)
                at = base_at + (t * share + c) * width
                pbuf[pl.ds(at, width), :] = jnp.where(live, base, 0.0)
                pbuf[pl.ds(flat + at, width), :] = jnp.where(live, scale, 0.0)

        loop(0, share // 2, direct, unroll=4)

    def finish(e):
        _, t, a0, before = ring(subs - 2, e)
        before.wait_recv()

        def some(i):
            for u in range(4):
                a = a0 + 4 * i + u
                total = part[t, sub, a].astype(F32) + recv[subs - 2, t, a].astype(F32)
                pbuf[pl.ds(t * share * stride + a, share, stride=stride), :] = total

        loop(0, rows_p // 4, some, unroll=rows_p // 4)

    def update(t, c):
        at = base_at + (t * share + c) * width
        out_ref[t, c] = (
            pbuf[pl.ds(at, width), :]
            + pbuf[pl.ds(flat + at, width), :] * pbuf[pl.ds((t * share + c) * stride, width), :]
        ).astype(BF16)

    for side in range(2):
        mask_copy(side).wait_send()
        for j in range(ZP):
            shift(side, j).wait_send()
    for i in range(1, planes):
        ids_copy(i, plane).wait_send()
        pair_copy(i, plane).wait_send()
    for i in range(1, Z):
        ids_copy_z(i, z).wait_send()
        pair_copy_z(i, z).wait_send()
    for i in range(1, subs):
        rows_copy(i, sub).wait_send()
    for step in range(subs - 2):
        loop(0, pieces, lambda e: ring(step, e)[3].wait_send())

    for t in range(tri):
        loop(t * each, (t + 1) * each, finish)
        loop(0, share, functools.partial(update, t), unroll=2)
    loop(0, pieces, lambda e: ring(subs - 2, e)[3].wait_send())


def local(
    amplitudes,
    tno_size,
    pair_amps,
    integrals,
    pair_intersection,
    nbr_intersection,
    tno_energy,
    lmo_energy,
    triples,
    pair_ids,
    nbr_ids,
    nbr_fock,
):
    tri, share, width, _ = amplitudes.shape
    nbrs = nbr_ids.shape[1]
    owned = pair_amps.shape[0]
    strips = lax.axis_size("strip")
    subs = lax.axis_size("sub")
    pieces = tri * 2 * AP
    smem = pl.BlockSpec(memory_space=pltpu.SMEM)
    vmem = pl.BlockSpec(memory_space=pltpu.VMEM)
    far = pl.BlockSpec(memory_space=pl.ANY)
    dma = pltpu.SemaphoreType.DMA
    return pl.pallas_call(
        functools.partial(kernel, strips, subs, tri, nbrs, share, width, owned),
        out_shape=jax.ShapeDtypeStruct(amplitudes.shape, BF16),
        in_specs=[smem] * 7 + [vmem] + [far] * 5,
        out_specs=vmem,
        scratch_shapes=[
            *[pltpu.VMEM((2 * tri, share // ZP, width, width), BF16) for _ in range(ZP)],
            pltpu.VMEM((tri * nbrs * share * (width + STRIDE_PAD), width), F32),
            pltpu.VMEM((tri, subs, width, share, width), BF16),
            pltpu.VMEM((subs - 1, tri, width, share, width), BF16),
            pltpu.VMEM(integrals.shape, BF16),
            pltpu.VMEM(amplitudes.shape, BF16),
            pltpu.VMEM(pair_amps.shape, BF16),
            pltpu.VMEM(pair_intersection.shape, BF16),
            pltpu.VMEM(nbr_intersection.shape, BF16),
            pltpu.VMEM((tri * nbrs, width, width), BF16),
            pltpu.VMEM((tri, width, width), BF16),
            pltpu.VMEM((tri, 8, width), F32),
            pltpu.VMEM((2 * tri, 8, width), F32),
            pltpu.VMEM((1, width), jnp.int32),
            pltpu.VMEM((strips, 1, width), jnp.int32),
            pltpu.SMEM((strips, 1, width), jnp.int32),
            pltpu.VMEM((strips // Z, Z, CAP, share, width), BF16),
            pltpu.VMEM((strips // Z, Z, CAP, share, width), BF16),
            pltpu.VMEM((Z, tri * 3, share, width), BF16),
            pltpu.VMEM((Z, tri * 3, share, width), BF16),
            pltpu.VMEM((tri * 3, share, width), BF16),
            pltpu.VMEM((subs, tri * 3, share, width), BF16),
            dma((5,)),
            dma((2,)),
            dma((2,)),
            dma,
            dma((strips // Z,)),
            dma((strips // Z,)),
            dma((2, ZP)),
            dma((2, ZP)),
            dma((Z,)),
            dma((Z,)),
            dma((strips // Z,)),
            dma((strips // Z,)),
            dma((Z,)),
            dma((Z,)),
            dma((subs,)),
            dma((subs,)),
            dma((subs - 1, pieces)),
            dma((subs - 1, pieces)),
        ],
        compiler_params=pltpu.CompilerParams(
            collective_id=0, has_side_effects=True, vmem_limit_bytes=60 * 1024 * 1024
        ),
    )(
        tno_size, pair_ids, nbr_ids, nbr_fock, triples, lmo_energy, tno_energy,
        tno_energy, amplitudes, pair_amps, integrals, pair_intersection, nbr_intersection,
    )


def solution(mesh):
    in_specs = (
        P("strip", "sub", None, None),
        P("strip"),
        P("strip", "sub", None),
        P("strip", None, "sub", None, None),
        P("strip", None, None, None),
        P("strip", None, None, None),
        P("strip", None),
        P(),
        P("strip", None),
        P("strip", None),
        P("strip", None),
        P("strip", None),
    )
    out_specs = P("strip", "sub", None, None)
    return jax.shard_map(local, mesh=mesh, in_specs=in_specs, out_specs=out_specs, check_vma=False)
```

```python
import functools

import jax
import jax.numpy as jnp
from jax import lax
from jax.experimental import pallas as pl
from jax.experimental.pallas import tpu as pltpu
from jax.sharding import PartitionSpec as P

MESH = pl.DeviceIdType.MESH
F32 = jnp.float32
BF16 = jnp.bfloat16
ZS = (8, 8, 8, 4, 4)
Z0 = (0, 8, 16, 24, 28)
ZP = len(ZS)
AP = 4
CAP = 2
Z = 8
CORES = 2
STRIDE_PAD = 8


def kernel(
    strips, subs, tri, nbrs, share, width, owned,
    size_ref, pair_ids_ref, nbr_ids_ref, fock_ref, triples_ref, lmo_ref, energy_ref,
    energy_rows_ref, amp_ref, pairs_ref, ints_ref, over_ref, inter_ref,
    result_ref,
    held0, held1, held2, held3, held4, pbuf, part, recv, ints, amp, pairs, over, s_raw, s_mask, w_all,
    masks_out, masks_in, ids_out, ids_all, ids_smem, staging, got, staging_z, got_z, mine, blocks, out_ref,
    local_sem, out_sem, mask_send, mask_recv, ids_sem, ids_send, ids_recv, shift_send, shift_recv,
    ids_send_z, ids_recv_z, pair_send, pair_recv, pair_send_z, pair_recv_z, rows_send, rows_recv, ring_send, ring_recv,
):
    strip = lax.axis_index("strip")
    sub = lax.axis_index("sub")
    up = lax.rem(strip + 1, strips)
    down = lax.rem(strip + strips - 1, strips)
    planes = strips // Z
    z = lax.rem(lax.div(strip, CORES), Z)
    plane = lax.div(strip, Z * CORES) * CORES + lax.rem(strip, CORES)
    far_side = jnp.where(lax.rem(strip, CORES) == 0, down, up)

    def strip_at(plane, z):
        return (lax.div(plane, CORES) * Z + z) * CORES + lax.rem(plane, CORES)

    stride = width + STRIDE_PAD
    rows_p = width // 2 // AP
    k = nbrs * share
    wants = tri * 3
    flat = tri * share * width
    base_at = tri * share * stride

    held = (held0, held1, held2, held3, held4)
    loads = [
        pltpu.make_async_copy(src, dst, local_sem.at[i])
        for i, (src, dst) in enumerate(
            [(inter_ref, s_raw), (pairs_ref, pairs), (over_ref, over), (amp_ref, amp), (ints_ref, ints)]
        )
    ]
    for copy in loads:
        copy.start()

    barrier = pltpu.get_barrier_semaphore()

    greeted = [(strip_at(lax.rem(plane + i, planes), z), sub) for i in range(1, planes)]
    greeted += [(strip_at(plane, lax.rem(z + i, Z)), sub) for i in range(1, Z)]
    greeted += [(strip, lax.rem(sub + i, subs)) for i in range(1, subs)]
    greeted += [(far_side, sub)]
    for device in greeted:
        pl.semaphore_signal(barrier, inc=1, device_id=device, device_id_type=MESH)

    lane = lax.broadcasted_iota(jnp.int32, (1, width), 1)
    for t in range(tri):
        size = size_ref[t]
        masks_out[t, 0:1] = jnp.where(lane < size, 1.0, 0.0).astype(F32)
        masks_out[t, 1:2] = jnp.where(lax.rem(lane, share) + sub * share < size, 1.0, 0.0).astype(F32)
        masks_out[t, 2:8] = jnp.zeros((6, width), F32)
    row = jnp.zeros((1, width), jnp.int32)
    for r in range(wants):
        row = jnp.where(lane == r, pair_ids_ref[r // 3, r % 3], row)
    ids_out[...] = row
    pl.semaphore_wait(barrier, len(greeted))

    def mask_copy(side):
        return pltpu.make_async_remote_copy(
            src_ref=masks_out,
            dst_ref=masks_in.at[pl.ds(side * tri, tri)],
            send_sem=mask_send.at[side],
            recv_sem=mask_recv.at[side],
            device_id=((up if side == 0 else down), sub),
            device_id_type=MESH,
        )

    def shift(side, j):
        return pltpu.make_async_remote_copy(
            src_ref=amp_ref.at[:, pl.ds(Z0[j], ZS[j])],
            dst_ref=held[j].at[pl.ds(side * tri, tri)],
            send_sem=shift_send.at[side, j],
            recv_sem=shift_recv.at[side, j],
            device_id=((up if side == 0 else down), sub),
            device_id_type=MESH,
        )

    def ids_copy(i, origin):
        return pltpu.make_async_remote_copy(
            src_ref=ids_out,
            dst_ref=ids_all.at[z * planes + origin],
            send_sem=ids_send.at[i],
            recv_sem=ids_recv.at[origin],
            device_id=(strip_at(lax.rem(plane + i, planes), z), sub),
            device_id_type=MESH,
        )

    def ids_copy_z(i, origin):
        return pltpu.make_async_remote_copy(
            src_ref=ids_all.at[pl.ds(z * planes, planes)],
            dst_ref=ids_all.at[pl.ds(origin * planes, planes)],
            send_sem=ids_send_z.at[i],
            recv_sem=ids_recv_z.at[origin],
            device_id=(strip_at(plane, lax.rem(z + i, Z)), sub),
            device_id_type=MESH,
        )

    def pair_copy(i, origin):
        other = lax.rem(plane + i, planes)
        return pltpu.make_async_remote_copy(
            src_ref=staging.at[other],
            dst_ref=got.at[origin],
            send_sem=pair_send.at[i],
            recv_sem=pair_recv.at[origin],
            device_id=(strip_at(other, z), sub),
            device_id_type=MESH,
        )

    def pair_copy_z(i, origin):
        other = lax.rem(z + i, Z)
        return pltpu.make_async_remote_copy(
            src_ref=staging_z.at[other],
            dst_ref=got_z.at[origin],
            send_sem=pair_send_z.at[i],
            recv_sem=pair_recv_z.at[origin],
            device_id=(strip_at(plane, other), sub),
            device_id_type=MESH,
        )

    def rows_copy(i, origin):
        return pltpu.make_async_remote_copy(
            src_ref=mine,
            dst_ref=blocks.at[origin],
            send_sem=rows_send.at[i],
            recv_sem=rows_recv.at[origin],
            device_id=(strip, lax.rem(sub + i, subs)),
            device_id_type=MESH,
        )

    def loop(first, last, body, unroll=1):
        def step(i, carry):
            body(i)
            return carry

        lax.fori_loop(first, last, step, 0, unroll=unroll)

    for side in range(2):
        mask_copy(side).start()
    for i in range(1, planes):
        ids_copy(i, plane).start()
    for j in range(2):
        for side in range(2):
            shift(side, j).start()
    ids_all[z * planes + plane] = ids_out[...]

    loads[0].wait()
    for side in range(2):
        mask_copy(side).wait_recv()

    def slot_of(i):
        place = nbr_ids_ref[i // nbrs, i % nbrs] - (strip - 1) * tri
        return jnp.clip(jnp.where(place >= 2 * tri, place - tri, place), 0, 2 * tri - 1)

    zr = lax.broadcasted_iota(jnp.int32, (width, width), 0)
    zc = lax.broadcasted_iota(jnp.int32, (width, width), 1)
    for t in range(tri):
        w = jnp.zeros((width, width), F32)
        factor = jnp.zeros((1, width), F32)
        for n in range(nbrs):
            i = t * nbrs + n
            mask = masks_in[slot_of(i)]
            raw = s_raw[t, n]
            s_mask[i] = (raw.astype(F32) * mask[0:1]).astype(BF16)
            choose = (zc // share == n) & (zr == lax.rem(zc, share) + sub * share)
            w = w + jnp.dot(raw, jnp.where(choose, 1.0, 0.0).astype(BF16), preferred_element_type=F32)
            factor = jnp.where(lane // share == n, mask[1:2] * fock_ref[t, n], factor)
        w_all[t] = (w * factor).astype(BF16)

    def project(j):
        zs = ZS[j]
        for side in range(2):
            shift(side, j).wait_recv()

        def pair(i):
            slot = slot_of(i)
            s = s_mask[i]
            halves = []
            for q in range(zs // 2):
                m = held[j][slot, pl.ds(2 * q, 2)]
                both = jnp.concatenate([m[0], m[1]], axis=1)
                h = jnp.dot(s, both, preferred_element_type=F32).astype(BF16)
                halves += [h[:, :width], h[:, width:]]
            full = jnp.concatenate(halves, axis=0)
            p = lax.dot_general(full, s, (((1,), (1,)), ((), ())), preferred_element_type=F32)
            for q in range(zs):
                pbuf[pl.ds((i * share + Z0[j] + q) * stride, width), :] = p[q * width:(q + 1) * width]

        loop(0, tri * nbrs, pair, unroll=tri * nbrs)

    for i in range(1, planes):
        ids_copy(i, lax.rem(plane + planes - i, planes)).wait_recv()
    for i in range(1, Z):
        ids_copy_z(i, z).start()
    for side in range(2):
        shift(side, 2).start()
    project(0)
    for j in range(3, ZP):
        for side in range(2):
            shift(side, j).start()

    loads[1].wait()
    for i in range(1, Z):
        ids_copy_z(i, lax.rem(z + Z - i, Z)).wait_recv()
    to_smem = pltpu.make_async_copy(ids_all, ids_smem, ids_sem)
    to_smem.start()
    to_smem.wait()

    def stage(m):
        count = jnp.int32(0)
        picks = [jnp.int32(0)] * CAP
        for r in range(wants):
            place = ids_smem[m, 0, r] - strip * owned
            here = (place >= 0) & (place < owned)
            for j in range(CAP):
                picks[j] = jnp.where(here & (count == j), place, picks[j])
            count = count + jnp.where(here, 1, 0)
        for j in range(CAP):
            staging[lax.rem(m, planes), lax.div(m, planes), j] = pairs[picks[j]]

    loop(0, strips, stage)
    for i in range(1, planes):
        pair_copy(i, plane).start()
    got[plane] = staging[plane]
    for j in range(1, ZP):
        project(j)

    def ring(step, e):
        way = lax.rem(e, 2)
        t = e // (2 * AP)
        p = lax.rem(e // 2, AP)
        sign = 1 - 2 * way
        chunk = lax.rem(sub - sign * (1 + step) + 2 * subs, subs)
        a0 = way * (width // 2) + p * rows_p
        return chunk, t, a0, pltpu.make_async_remote_copy(
            src_ref=part.at[t, chunk, pl.ds(a0, rows_p)],
            dst_ref=recv.at[step, t, pl.ds(a0, rows_p)],
            send_sem=ring_send.at[step, e],
            recv_sem=ring_recv.at[step, e],
            device_id=(strip, lax.rem(sub + sign + subs, subs)),
            device_id_type=MESH,
        )

    each = 2 * AP
    pieces = tri * each

    def couple(e):
        chunk, t, a0, copy = ring(0, e)

        def some(i):
            a = a0 + 4 * i
            w = w_all[t][:, :k]
            for v in range(2):
                both = jnp.concatenate(
                    [
                        pbuf[pl.ds(t * k * stride + a + 2 * v + u, k, stride=stride), :].astype(BF16)
                        for u in range(2)
                    ],
                    axis=1,
                )
                o = jnp.dot(w, both, preferred_element_type=F32).astype(BF16)
                for u in range(2):
                    for d in range(subs):
                        part[t, d, a + 2 * v + u] = o[d * share:(d + 1) * share, u * width:(u + 1) * width]

        loop(0, rows_p // 4, some, unroll=rows_p // 4)
        copy.start()

    loop(0, each, couple)
    for i in range(1, planes):
        pair_copy(i, lax.rem(plane + planes - i, planes)).wait_recv()

    def merge(other):
        owners = [lax.div(ids_smem[other * planes + plane, 0, r], owned) for r in range(wants)]
        for r in range(wants):
            rank = jnp.int32(0)
            for q in range(r):
                rank = rank + jnp.where(owners[q] == owners[r], 1, 0)
            source = lax.div(owners[r], Z * CORES) * CORES + lax.rem(owners[r], CORES)
            staging_z[other, r] = got[source, other, jnp.minimum(rank, CAP - 1)]

    loop(0, Z, merge)
    for i in range(1, Z):
        pair_copy_z(i, z).start()
    got_z[z] = staging_z[z]
    loop(each, pieces, couple)

    def onward(step, e):
        _, _, _, before = ring(step - 1, e)
        chunk, t, a0, copy = ring(step, e)
        before.wait_recv()
        rows = pl.ds(a0, rows_p)
        total = part[t, chunk, rows].astype(F32) + recv[step - 1, t, rows].astype(F32)
        part[t, chunk, rows] = total.astype(BF16)
        copy.start()

    for step in range(1, subs - 1):
        loop(0, pieces, functools.partial(onward, step))
        if step == 1:
            for i in range(1, Z):
                pair_copy_z(i, lax.rem(z + Z - i, Z)).wait_recv()
            for r in range(wants):
                owner = lax.div(pair_ids_ref[r // 3, r % 3], owned)
                mine[r] = got_z[lax.rem(lax.div(owner, CORES), Z), r]
            for i in range(1, subs):
                rows_copy(i, sub).start()
            blocks[sub] = mine[...]

    loads[2].wait()
    loads[3].wait()
    loads[4].wait()
    for i in range(1, subs):
        rows_copy(i, lax.rem(sub + subs - i, subs)).wait_recv()
    for t in range(tri):
        tno = []
        for r in range(3):
            block = jnp.concatenate([blocks[y, t * 3 + r] for y in range(subs)], axis=0)
            o = over[t, r]
            left = jnp.dot(o, block, preferred_element_type=F32).astype(BF16)
            tno.append(
                lax.dot_general(left, o, (((1,), (1,)), ((), ())), preferred_element_type=F32).astype(BF16)
            )
        tno = jnp.concatenate(tno, axis=1)
        size = size_ref[t]
        live_ab = (zr < size) & (zc < size)
        energy_b = jnp.broadcast_to(energy_rows_ref[t:t + 1], (width, width))
        lmo_total = lmo_ref[triples_ref[t, 0]] + lmo_ref[triples_ref[t, 1]] + lmo_ref[triples_ref[t, 2]]
        den_ab = energy_b.T + energy_b - lmo_total

        def direct(v, t=t, tno=tno, size=size, live_ab=live_ab, den_ab=den_ab):
            both = jnp.concatenate(
                [
                    jnp.concatenate([ints[t, r, 2 * v + u] for r in range(3)], axis=0)
                    for u in range(2)
                ],
                axis=1,
            )
            x = jnp.dot(tno, both, preferred_element_type=F32)
            for u in range(2):
                c = 2 * v + u
                xu = x[:, u * width:(u + 1) * width]
                wsum = xu + xu.T
                live = live_ab & (sub * share + c < size)
                current = amp[t, c].astype(F32)
                den = den_ab + energy_ref[t, sub * share + c]
                scale = 0.7 / den
                base = current - scale * (wsum + den * current)
                at = base_at + (t * share + c) * width
                pbuf[pl.ds(at, width), :] = jnp.where(live, base, 0.0)
                pbuf[pl.ds(flat + at, width), :] = jnp.where(live, scale, 0.0)

        loop(0, share // 2, direct, unroll=4)

    def finish(e):
        _, t, a0, before = ring(subs - 2, e)
        before.wait_recv()

        def some(i):
            for u in range(4):
                a = a0 + 4 * i + u
                total = part[t, sub, a].astype(F32) + recv[subs - 2, t, a].astype(F32)
                pbuf[pl.ds(t * share * stride + a, share, stride=stride), :] = total

        loop(0, rows_p // 4, some, unroll=rows_p // 4)

    def update(t, c):
        at = base_at + (t * share + c) * width
        out_ref[t, c] = (
            pbuf[pl.ds(at, width), :]
            + pbuf[pl.ds(flat + at, width), :] * pbuf[pl.ds((t * share + c) * stride, width), :]
        ).astype(BF16)

    for side in range(2):
        mask_copy(side).wait_send()
        for j in range(ZP):
            shift(side, j).wait_send()
    for i in range(1, planes):
        ids_copy(i, plane).wait_send()
        pair_copy(i, plane).wait_send()
    for i in range(1, Z):
        ids_copy_z(i, z).wait_send()
        pair_copy_z(i, z).wait_send()
    for i in range(1, subs):
        rows_copy(i, sub).wait_send()
    for step in range(subs - 2):
        loop(0, pieces, lambda e: ring(step, e)[3].wait_send())

    half = share // 2

    def write(t, h):
        rows = pl.ds(h * half, half)
        return pltpu.make_async_copy(out_ref.at[t, rows], result_ref.at[t, rows], out_sem.at[t, h])

    for t in range(tri):
        loop(t * each, (t + 1) * each, finish)
        for h in range(2):
            loop(h * half, (h + 1) * half, functools.partial(update, t), unroll=4)
            write(t, h).start()
    loop(0, pieces, lambda e: ring(subs - 2, e)[3].wait_send())
    for t in range(tri):
        for h in range(2):
            write(t, h).wait()


def local(
    amplitudes,
    tno_size,
    pair_amps,
    integrals,
    pair_intersection,
    nbr_intersection,
    tno_energy,
    lmo_energy,
    triples,
    pair_ids,
    nbr_ids,
    nbr_fock,
):
    tri, share, width, _ = amplitudes.shape
    nbrs = nbr_ids.shape[1]
    owned = pair_amps.shape[0]
    strips = lax.axis_size("strip")
    subs = lax.axis_size("sub")
    pieces = tri * 2 * AP
    smem = pl.BlockSpec(memory_space=pltpu.SMEM)
    vmem = pl.BlockSpec(memory_space=pltpu.VMEM)
    far = pl.BlockSpec(memory_space=pl.ANY)
    dma = pltpu.SemaphoreType.DMA
    return pl.pallas_call(
        functools.partial(kernel, strips, subs, tri, nbrs, share, width, owned),
        out_shape=jax.ShapeDtypeStruct(amplitudes.shape, BF16),
        in_specs=[smem] * 7 + [vmem] + [far] * 5,
        out_specs=far,
        scratch_shapes=[
            *[pltpu.VMEM((2 * tri, rows, width, width), BF16) for rows in ZS],
            pltpu.VMEM((tri * nbrs * share * (width + STRIDE_PAD), width), F32),
            pltpu.VMEM((tri, subs, width, share, width), BF16),
            pltpu.VMEM((subs - 1, tri, width, share, width), BF16),
            pltpu.VMEM(integrals.shape, BF16),
            pltpu.VMEM(amplitudes.shape, BF16),
            pltpu.VMEM(pair_amps.shape, BF16),
            pltpu.VMEM(pair_intersection.shape, BF16),
            pltpu.VMEM(nbr_intersection.shape, BF16),
            pltpu.VMEM((tri * nbrs, width, width), BF16),
            pltpu.VMEM((tri, width, width), BF16),
            pltpu.VMEM((tri, 8, width), F32),
            pltpu.VMEM((2 * tri, 8, width), F32),
            pltpu.VMEM((1, width), jnp.int32),
            pltpu.VMEM((strips, 1, width), jnp.int32),
            pltpu.SMEM((strips, 1, width), jnp.int32),
            pltpu.VMEM((strips // Z, Z, CAP, share, width), BF16),
            pltpu.VMEM((strips // Z, Z, CAP, share, width), BF16),
            pltpu.VMEM((Z, tri * 3, share, width), BF16),
            pltpu.VMEM((Z, tri * 3, share, width), BF16),
            pltpu.VMEM((tri * 3, share, width), BF16),
            pltpu.VMEM((subs, tri * 3, share, width), BF16),
            pltpu.VMEM(amplitudes.shape, BF16),
            dma((5,)),
            dma((tri, 2)),
            dma((2,)),
            dma((2,)),
            dma,
            dma((strips // Z,)),
            dma((strips // Z,)),
            dma((2, ZP)),
            dma((2, ZP)),
            dma((Z,)),
            dma((Z,)),
            dma((strips // Z,)),
            dma((strips // Z,)),
            dma((Z,)),
            dma((Z,)),
            dma((subs,)),
            dma((subs,)),
            dma((subs - 1, pieces)),
            dma((subs - 1, pieces)),
        ],
        compiler_params=pltpu.CompilerParams(
            collective_id=0, has_side_effects=True, vmem_limit_bytes=60 * 1024 * 1024
        ),
    )(
        tno_size, pair_ids, nbr_ids, nbr_fock, triples, lmo_energy, tno_energy,
        tno_energy, amplitudes, pair_amps, integrals, pair_intersection, nbr_intersection,
    )


def solution(mesh):
    in_specs = (
        P("strip", "sub", None, None),
        P("strip"),
        P("strip", "sub", None),
        P("strip", None, "sub", None, None),
        P("strip", None, None, None),
        P("strip", None, None, None),
        P("strip", None),
        P(),
        P("strip", None),
        P("strip", None),
        P("strip", None),
        P("strip", None),
    )
    out_specs = P("strip", "sub", None, None)
    return jax.shard_map(local, mesh=mesh, in_specs=in_specs, out_specs=out_specs, check_vma=False)
```

```python
import functools

import jax
import jax.numpy as jnp
from jax import lax
from jax.experimental import pallas as pl
from jax.experimental.pallas import tpu as pltpu
from jax.sharding import PartitionSpec as P

MESH = pl.DeviceIdType.MESH
F32 = jnp.float32
BF16 = jnp.bfloat16
ZS = (8, 8, 8, 4, 4)
Z0 = (0, 8, 16, 24, 28)
ZP = len(ZS)
AP = 4
CAP = 2
Z = 8
CORES = 2
STRIDE_PAD = 8


def kernel(
    strips, subs, tri, nbrs, share, width, owned,
    size_ref, pair_ids_ref, nbr_ids_ref, fock_ref, triples_ref, lmo_ref, energy_ref,
    energy_rows_ref, amp_ref, pairs_ref, ints_ref, over_ref, inter_ref,
    out_ref,
    held0, held1, held2, held3, held4, pbuf, part, recv, ints, amp, pairs, over, s_raw, s_mask, w_all,
    masks_out, masks_in, ids_out, ids_all, ids_smem, staging, got, staging_z, got_z, mine, blocks,
    local_sem, mask_send, mask_recv, ids_sem, ids_send, ids_recv, shift_send, shift_recv,
    ids_send_z, ids_recv_z, pair_send, pair_recv, pair_send_z, pair_recv_z, rows_send, rows_recv, ring_send, ring_recv,
):
    strip = lax.axis_index("strip")
    sub = lax.axis_index("sub")
    up = lax.rem(strip + 1, strips)
    down = lax.rem(strip + strips - 1, strips)
    planes = strips // Z
    z = lax.rem(lax.div(strip, CORES), Z)
    plane = lax.div(strip, Z * CORES) * CORES + lax.rem(strip, CORES)
    far_side = jnp.where(lax.rem(strip, CORES) == 0, down, up)

    def strip_at(plane, z):
        return (lax.div(plane, CORES) * Z + z) * CORES + lax.rem(plane, CORES)

    stride = width + STRIDE_PAD
    rows_p = width // 2 // AP
    k = nbrs * share
    wants = tri * 3
    flat = tri * share * width
    base_at = tri * share * stride

    held = (held0, held1, held2, held3, held4)
    loads = [
        pltpu.make_async_copy(src, dst, local_sem.at[i])
        for i, (src, dst) in enumerate(
            [(inter_ref, s_raw), (pairs_ref, pairs), (over_ref, over), (amp_ref, amp), (ints_ref, ints)]
        )
    ]
    for copy in loads:
        copy.start()

    barrier = pltpu.get_barrier_semaphore()

    greeted = [(strip_at(lax.rem(plane + i, planes), z), sub) for i in range(1, planes)]
    greeted += [(strip_at(plane, lax.rem(z + i, Z)), sub) for i in range(1, Z)]
    greeted += [(strip, lax.rem(sub + i, subs)) for i in range(1, subs)]
    greeted += [(far_side, sub)]
    for device in greeted:
        pl.semaphore_signal(barrier, inc=1, device_id=device, device_id_type=MESH)

    lane = lax.broadcasted_iota(jnp.int32, (1, width), 1)
    for t in range(tri):
        size = size_ref[t]
        masks_out[t, 0:1] = jnp.where(lane < size, 1.0, 0.0).astype(F32)
        masks_out[t, 1:2] = jnp.where(lax.rem(lane, share) + sub * share < size, 1.0, 0.0).astype(F32)
        masks_out[t, 2:8] = jnp.zeros((6, width), F32)
    row = jnp.zeros((1, width), jnp.int32)
    for r in range(wants):
        row = jnp.where(lane == r, pair_ids_ref[r // 3, r % 3], row)
    ids_out[...] = row
    pl.semaphore_wait(barrier, len(greeted))

    def mask_copy(side):
        return pltpu.make_async_remote_copy(
            src_ref=masks_out,
            dst_ref=masks_in.at[pl.ds(side * tri, tri)],
            send_sem=mask_send.at[side],
            recv_sem=mask_recv.at[side],
            device_id=((up if side == 0 else down), sub),
            device_id_type=MESH,
        )

    def shift(side, j):
        return pltpu.make_async_remote_copy(
            src_ref=amp_ref.at[:, pl.ds(Z0[j], ZS[j])],
            dst_ref=held[j].at[pl.ds(side * tri, tri)],
            send_sem=shift_send.at[side, j],
            recv_sem=shift_recv.at[side, j],
            device_id=((up if side == 0 else down), sub),
            device_id_type=MESH,
        )

    def ids_copy(i, origin):
        return pltpu.make_async_remote_copy(
            src_ref=ids_out,
            dst_ref=ids_all.at[z * planes + origin],
            send_sem=ids_send.at[i],
            recv_sem=ids_recv.at[origin],
            device_id=(strip_at(lax.rem(plane + i, planes), z), sub),
            device_id_type=MESH,
        )

    def ids_copy_z(i, origin):
        return pltpu.make_async_remote_copy(
            src_ref=ids_all.at[pl.ds(z * planes, planes)],
            dst_ref=ids_all.at[pl.ds(origin * planes, planes)],
            send_sem=ids_send_z.at[i],
            recv_sem=ids_recv_z.at[origin],
            device_id=(strip_at(plane, lax.rem(z + i, Z)), sub),
            device_id_type=MESH,
        )

    def pair_copy(i, origin):
        other = lax.rem(plane + i, planes)
        return pltpu.make_async_remote_copy(
            src_ref=staging.at[other],
            dst_ref=got.at[origin],
            send_sem=pair_send.at[i],
            recv_sem=pair_recv.at[origin],
            device_id=(strip_at(other, z), sub),
            device_id_type=MESH,
        )

    def pair_copy_z(i, origin):
        other = lax.rem(z + i, Z)
        return pltpu.make_async_remote_copy(
            src_ref=staging_z.at[other],
            dst_ref=got_z.at[origin],
            send_sem=pair_send_z.at[i],
            recv_sem=pair_recv_z.at[origin],
            device_id=(strip_at(plane, other), sub),
            device_id_type=MESH,
        )

    def rows_copy(i, origin):
        return pltpu.make_async_remote_copy(
            src_ref=mine,
            dst_ref=blocks.at[origin],
            send_sem=rows_send.at[i],
            recv_sem=rows_recv.at[origin],
            device_id=(strip, lax.rem(sub + i, subs)),
            device_id_type=MESH,
        )

    def loop(first, last, body, unroll=1):
        def step(i, carry):
            body(i)
            return carry

        lax.fori_loop(first, last, step, 0, unroll=unroll)

    for side in range(2):
        mask_copy(side).start()
    for i in range(1, planes):
        ids_copy(i, plane).start()
    for j in range(2):
        for side in range(2):
            shift(side, j).start()
    ids_all[z * planes + plane] = ids_out[...]

    loads[0].wait()
    for side in range(2):
        mask_copy(side).wait_recv()

    def slot_of(i):
        place = nbr_ids_ref[i // nbrs, i % nbrs] - (strip - 1) * tri
        return jnp.clip(jnp.where(place >= 2 * tri, place - tri, place), 0, 2 * tri - 1)

    zr = lax.broadcasted_iota(jnp.int32, (width, width), 0)
    zc = lax.broadcasted_iota(jnp.int32, (width, width), 1)
    for t in range(tri):
        w = jnp.zeros((width, width), F32)
        factor = jnp.zeros((1, width), F32)
        for n in range(nbrs):
            i = t * nbrs + n
            mask = masks_in[slot_of(i)]
            raw = s_raw[t, n]
            s_mask[i] = (raw.astype(F32) * mask[0:1]).astype(BF16)
            choose = (zc // share == n) & (zr == lax.rem(zc, share) + sub * share)
            w = w + jnp.dot(raw, jnp.where(choose, 1.0, 0.0).astype(BF16), preferred_element_type=F32)
            factor = jnp.where(lane // share == n, mask[1:2] * fock_ref[t, n], factor)
        w_all[t] = (w * factor).astype(BF16)

    def project(j):
        zs = ZS[j]
        for side in range(2):
            shift(side, j).wait_recv()

        def pair(i):
            slot = slot_of(i)
            s = s_mask[i]
            halves = []
            for q in range(zs // 2):
                m = held[j][slot, pl.ds(2 * q, 2)]
                both = jnp.concatenate([m[0], m[1]], axis=1)
                h = jnp.dot(s, both, preferred_element_type=F32).astype(BF16)
                halves += [h[:, :width], h[:, width:]]
            full = jnp.concatenate(halves, axis=0)
            p = lax.dot_general(full, s, (((1,), (1,)), ((), ())), preferred_element_type=F32)
            for q in range(zs):
                pbuf[pl.ds((i * share + Z0[j] + q) * stride, width), :] = p[q * width:(q + 1) * width]

        loop(0, tri * nbrs, pair, unroll=tri * nbrs)

    for i in range(1, planes):
        ids_copy(i, lax.rem(plane + planes - i, planes)).wait_recv()
    for i in range(1, Z):
        ids_copy_z(i, z).start()
    for side in range(2):
        shift(side, 2).start()
    project(0)
    for j in range(3, ZP):
        for side in range(2):
            shift(side, j).start()

    loads[1].wait()
    for i in range(1, Z):
        ids_copy_z(i, lax.rem(z + Z - i, Z)).wait_recv()
    to_smem = pltpu.make_async_copy(ids_all, ids_smem, ids_sem)
    to_smem.start()
    to_smem.wait()

    def stage(m):
        count = jnp.int32(0)
        picks = [jnp.int32(0)] * CAP
        for r in range(wants):
            place = ids_smem[m, 0, r] - strip * owned
            here = (place >= 0) & (place < owned)
            for j in range(CAP):
                picks[j] = jnp.where(here & (count == j), place, picks[j])
            count = count + jnp.where(here, 1, 0)
        for j in range(CAP):
            staging[lax.rem(m, planes), lax.div(m, planes), j] = pairs[picks[j]]

    loop(0, strips, stage)
    for i in range(1, planes):
        pair_copy(i, plane).start()
    got[plane] = staging[plane]
    for j in range(1, ZP):
        project(j)

    def ring(step, e):
        way = lax.rem(e, 2)
        t = e // (2 * AP)
        p = lax.rem(e // 2, AP)
        sign = 1 - 2 * way
        chunk = lax.rem(sub - sign * (1 + step) + 2 * subs, subs)
        a0 = way * (width // 2) + p * rows_p
        return chunk, t, a0, pltpu.make_async_remote_copy(
            src_ref=part.at[t, chunk, pl.ds(a0, rows_p)],
            dst_ref=recv.at[step, t, pl.ds(a0, rows_p)],
            send_sem=ring_send.at[step, e],
            recv_sem=ring_recv.at[step, e],
            device_id=(strip, lax.rem(sub + sign + subs, subs)),
            device_id_type=MESH,
        )

    each = 2 * AP
    pieces = tri * each

    def couple(e):
        chunk, t, a0, copy = ring(0, e)

        def some(i):
            a = a0 + 4 * i
            w = w_all[t][:, :k]
            for v in range(2):
                both = jnp.concatenate(
                    [
                        pbuf[pl.ds(t * k * stride + a + 2 * v + u, k, stride=stride), :].astype(BF16)
                        for u in range(2)
                    ],
                    axis=1,
                )
                o = jnp.dot(w, both, preferred_element_type=F32).astype(BF16)
                for u in range(2):
                    for d in range(subs):
                        part[t, d, a + 2 * v + u] = o[d * share:(d + 1) * share, u * width:(u + 1) * width]

        loop(0, rows_p // 4, some, unroll=rows_p // 4)
        copy.start()

    loop(0, each, couple)
    for i in range(1, planes):
        pair_copy(i, lax.rem(plane + planes - i, planes)).wait_recv()

    def merge(other):
        owners = [lax.div(ids_smem[other * planes + plane, 0, r], owned) for r in range(wants)]
        for r in range(wants):
            rank = jnp.int32(0)
            for q in range(r):
                rank = rank + jnp.where(owners[q] == owners[r], 1, 0)
            source = lax.div(owners[r], Z * CORES) * CORES + lax.rem(owners[r], CORES)
            staging_z[other, r] = got[source, other, jnp.minimum(rank, CAP - 1)]

    loop(0, Z, merge)
    for i in range(1, Z):
        pair_copy_z(i, z).start()
    got_z[z] = staging_z[z]
    loop(each, pieces, couple)

    def onward(step, e):
        _, _, _, before = ring(step - 1, e)
        chunk, t, a0, copy = ring(step, e)
        before.wait_recv()
        rows = pl.ds(a0, rows_p)
        total = part[t, chunk, rows].astype(F32) + recv[step - 1, t, rows].astype(F32)
        part[t, chunk, rows] = total.astype(BF16)
        copy.start()

    for step in range(1, subs - 1):
        loop(0, pieces, functools.partial(onward, step))
        if step == 1:
            for i in range(1, Z):
                pair_copy_z(i, lax.rem(z + Z - i, Z)).wait_recv()
            for r in range(wants):
                owner = lax.div(pair_ids_ref[r // 3, r % 3], owned)
                mine[r] = got_z[lax.rem(lax.div(owner, CORES), Z), r]
            for i in range(1, subs):
                rows_copy(i, sub).start()
            blocks[sub] = mine[...]

    loads[2].wait()
    loads[3].wait()
    loads[4].wait()
    for i in range(1, subs):
        rows_copy(i, lax.rem(sub + subs - i, subs)).wait_recv()
    for t in range(tri):
        tno = []
        for r in range(3):
            block = jnp.concatenate([blocks[y, t * 3 + r] for y in range(subs)], axis=0)
            o = over[t, r]
            left = jnp.dot(o, block, preferred_element_type=F32).astype(BF16)
            tno.append(
                lax.dot_general(left, o, (((1,), (1,)), ((), ())), preferred_element_type=F32).astype(BF16)
            )
        tno = jnp.concatenate(tno, axis=1)
        size = size_ref[t]
        live_ab = (zr < size) & (zc < size)
        energy_b = jnp.broadcast_to(energy_rows_ref[t:t + 1], (width, width))
        lmo_total = lmo_ref[triples_ref[t, 0]] + lmo_ref[triples_ref[t, 1]] + lmo_ref[triples_ref[t, 2]]
        den_ab = energy_b.T + energy_b - lmo_total

        def direct(v, t=t, tno=tno, size=size, live_ab=live_ab, den_ab=den_ab):
            both = jnp.concatenate(
                [
                    jnp.concatenate([ints[t, r, 2 * v + u] for r in range(3)], axis=0)
                    for u in range(2)
                ],
                axis=1,
            )
            x = jnp.dot(tno, both, preferred_element_type=F32)
            for u in range(2):
                c = 2 * v + u
                xu = x[:, u * width:(u + 1) * width]
                wsum = xu + xu.T
                live = live_ab & (sub * share + c < size)
                current = amp[t, c].astype(F32)
                den = den_ab + energy_ref[t, sub * share + c]
                scale = 0.7 / den
                base = current - scale * (wsum + den * current)
                at = base_at + (t * share + c) * width
                pbuf[pl.ds(at, width), :] = jnp.where(live, base, 0.0)
                pbuf[pl.ds(flat + at, width), :] = jnp.where(live, scale, 0.0)

        loop(0, share // 2, direct, unroll=4)

    def finish(e):
        _, t, a0, before = ring(subs - 2, e)
        before.wait_recv()

        def some(i):
            for u in range(4):
                a = a0 + 4 * i + u
                total = part[t, sub, a].astype(F32) + recv[subs - 2, t, a].astype(F32)
                pbuf[pl.ds(t * share * stride + a, share, stride=stride), :] = total

        loop(0, rows_p // 4, some, unroll=rows_p // 4)

    def update(t, c):
        at = base_at + (t * share + c) * width
        out_ref[t, c] = (
            pbuf[pl.ds(at, width), :]
            + pbuf[pl.ds(flat + at, width), :] * pbuf[pl.ds((t * share + c) * stride, width), :]
        ).astype(BF16)

    for side in range(2):
        mask_copy(side).wait_send()
        for j in range(ZP):
            shift(side, j).wait_send()
    for i in range(1, planes):
        ids_copy(i, plane).wait_send()
        pair_copy(i, plane).wait_send()
    for i in range(1, Z):
        ids_copy_z(i, z).wait_send()
        pair_copy_z(i, z).wait_send()
    for i in range(1, subs):
        rows_copy(i, sub).wait_send()
    for step in range(subs - 2):
        loop(0, pieces, lambda e: ring(step, e)[3].wait_send())

    for t in range(tri):
        loop(t * each, (t + 1) * each, finish)
        loop(0, share, functools.partial(update, t), unroll=4)
    loop(0, pieces, lambda e: ring(subs - 2, e)[3].wait_send())


def local(
    amplitudes,
    tno_size,
    pair_amps,
    integrals,
    pair_intersection,
    nbr_intersection,
    tno_energy,
    lmo_energy,
    triples,
    pair_ids,
    nbr_ids,
    nbr_fock,
):
    tri, share, width, _ = amplitudes.shape
    nbrs = nbr_ids.shape[1]
    owned = pair_amps.shape[0]
    strips = lax.axis_size("strip")
    subs = lax.axis_size("sub")
    pieces = tri * 2 * AP
    smem = pl.BlockSpec(memory_space=pltpu.SMEM)
    vmem = pl.BlockSpec(memory_space=pltpu.VMEM)
    far = pl.BlockSpec(memory_space=pltpu.HBM)
    dma = pltpu.SemaphoreType.DMA
    return pl.pallas_call(
        functools.partial(kernel, strips, subs, tri, nbrs, share, width, owned),
        out_shape=pltpu.VMEM(amplitudes.shape, BF16),
        in_specs=[smem] * 7 + [vmem] + [far] * 5,
        out_specs=vmem,
        scratch_shapes=[
            *[pltpu.VMEM((2 * tri, rows, width, width), BF16) for rows in ZS],
            pltpu.VMEM((tri * nbrs * share * (width + STRIDE_PAD), width), F32),
            pltpu.VMEM((tri, subs, width, share, width), BF16),
            pltpu.VMEM((subs - 1, tri, width, share, width), BF16),
            pltpu.VMEM(integrals.shape, BF16),
            pltpu.VMEM(amplitudes.shape, BF16),
            pltpu.VMEM(pair_amps.shape, BF16),
            pltpu.VMEM(pair_intersection.shape, BF16),
            pltpu.VMEM(nbr_intersection.shape, BF16),
            pltpu.VMEM((tri * nbrs, width, width), BF16),
            pltpu.VMEM((tri, width, width), BF16),
            pltpu.VMEM((tri, 8, width), F32),
            pltpu.VMEM((2 * tri, 8, width), F32),
            pltpu.VMEM((1, width), jnp.int32),
            pltpu.VMEM((strips, 1, width), jnp.int32),
            pltpu.SMEM((strips, 1, width), jnp.int32),
            pltpu.VMEM((strips // Z, Z, CAP, share, width), BF16),
            pltpu.VMEM((strips // Z, Z, CAP, share, width), BF16),
            pltpu.VMEM((Z, tri * 3, share, width), BF16),
            pltpu.VMEM((Z, tri * 3, share, width), BF16),
            pltpu.VMEM((tri * 3, share, width), BF16),
            pltpu.VMEM((subs, tri * 3, share, width), BF16),
            dma((5,)),
            dma((2,)),
            dma((2,)),
            dma,
            dma((strips // Z,)),
            dma((strips // Z,)),
            dma((2, ZP)),
            dma((2, ZP)),
            dma((Z,)),
            dma((Z,)),
            dma((strips // Z,)),
            dma((strips // Z,)),
            dma((Z,)),
            dma((Z,)),
            dma((subs,)),
            dma((subs,)),
            dma((subs - 1, pieces)),
            dma((subs - 1, pieces)),
        ],
        compiler_params=pltpu.CompilerParams(
            collective_id=0, has_side_effects=True, vmem_limit_bytes=56 * 1024 * 1024
        ),
    )(
        tno_size, pair_ids, nbr_ids, nbr_fock, triples, lmo_energy, tno_energy,
        tno_energy, amplitudes, pair_amps, integrals, pair_intersection, nbr_intersection,
    )


def solution(mesh):
    in_specs = (
        P("strip", "sub", None, None),
        P("strip"),
        P("strip", "sub", None),
        P("strip", None, "sub", None, None),
        P("strip", None, None, None),
        P("strip", None, None, None),
        P("strip", None),
        P(),
        P("strip", None),
        P("strip", None),
        P("strip", None),
        P("strip", None),
    )
    out_specs = P("strip", "sub", None, None)
    return jax.shard_map(local, mesh=mesh, in_specs=in_specs, out_specs=out_specs, check_vma=False)
```

```python
import functools

import jax
import jax.numpy as jnp
from jax import lax
from jax.experimental import pallas as pl
from jax.experimental.pallas import tpu as pltpu
from jax.sharding import PartitionSpec as P

MESH = pl.DeviceIdType.MESH
F32 = jnp.float32
BF16 = jnp.bfloat16
ZS = (8, 8, 8, 4, 4)
Z0 = (0, 8, 16, 24, 28)
ZP = len(ZS)
AP = 4
CAP = 2
Z = 8
CORES = 2
STRIDE_PAD = 8


def kernel(
    strips, subs, tri, nbrs, share, width, owned,
    size_ref, pair_ids_ref, nbr_ids_ref, fock_ref, triples_far, lmo_far, energy_far,
    energy_rows_ref, amp_ref, pairs_ref, ints_ref, over_ref, inter_ref,
    out_ref,
    held0, held1, held2, held3, held4, pbuf, part, recv, ints, amp, pairs, over, s_raw, s_mask, w_all,
    masks_out, masks_in, ids_out, ids_all, ids_smem, staging, got, staging_z, got_z, mine, blocks,
    triples_ref, lmo_ref, energy_ref, local_sem, mask_send, mask_recv, ids_sem, ids_send, ids_recv, shift_send, shift_recv,
    ids_send_z, ids_recv_z, pair_send, pair_recv, pair_send_z, pair_recv_z, rows_send, rows_recv, ring_send, ring_recv,
):
    strip = lax.axis_index("strip")
    sub = lax.axis_index("sub")
    up = lax.rem(strip + 1, strips)
    down = lax.rem(strip + strips - 1, strips)
    planes = strips // Z
    z = lax.rem(lax.div(strip, CORES), Z)
    plane = lax.div(strip, Z * CORES) * CORES + lax.rem(strip, CORES)
    far_side = jnp.where(lax.rem(strip, CORES) == 0, down, up)

    def strip_at(plane, z):
        return (lax.div(plane, CORES) * Z + z) * CORES + lax.rem(plane, CORES)

    stride = width + STRIDE_PAD
    rows_p = width // 2 // AP
    k = nbrs * share
    wants = tri * 3
    flat = tri * share * width
    base_at = tri * share * stride

    held = (held0, held1, held2, held3, held4)
    loads = [
        pltpu.make_async_copy(src, dst, local_sem.at[i])
        for i, (src, dst) in enumerate(
            [(inter_ref, s_raw), (pairs_ref, pairs), (over_ref, over), (amp_ref, amp), (ints_ref, ints),
             (triples_far, triples_ref), (lmo_far, lmo_ref), (energy_far, energy_ref)]
        )
    ]
    for copy in loads:
        copy.start()

    barrier = pltpu.get_barrier_semaphore()

    greeted = [(strip_at(lax.rem(plane + i, planes), z), sub) for i in range(1, planes)]
    greeted += [(strip_at(plane, lax.rem(z + i, Z)), sub) for i in range(1, Z)]
    greeted += [(strip, lax.rem(sub + i, subs)) for i in range(1, subs)]
    greeted += [(far_side, sub)]
    for device in greeted:
        pl.semaphore_signal(barrier, inc=1, device_id=device, device_id_type=MESH)

    lane = lax.broadcasted_iota(jnp.int32, (1, width), 1)
    for t in range(tri):
        size = size_ref[t]
        masks_out[t, 0:1] = jnp.where(lane < size, 1.0, 0.0).astype(F32)
        masks_out[t, 1:2] = jnp.where(lax.rem(lane, share) + sub * share < size, 1.0, 0.0).astype(F32)
        masks_out[t, 2:8] = jnp.zeros((6, width), F32)
    row = jnp.zeros((1, width), jnp.int32)
    for r in range(wants):
        row = jnp.where(lane == r, pair_ids_ref[r // 3, r % 3], row)
    ids_out[...] = row
    pl.semaphore_wait(barrier, len(greeted))

    def mask_copy(side):
        return pltpu.make_async_remote_copy(
            src_ref=masks_out,
            dst_ref=masks_in.at[pl.ds(side * tri, tri)],
            send_sem=mask_send.at[side],
            recv_sem=mask_recv.at[side],
            device_id=((up if side == 0 else down), sub),
            device_id_type=MESH,
        )

    def shift(side, j):
        return pltpu.make_async_remote_copy(
            src_ref=amp_ref.at[:, pl.ds(Z0[j], ZS[j])],
            dst_ref=held[j].at[pl.ds(side * tri, tri)],
            send_sem=shift_send.at[side, j],
            recv_sem=shift_recv.at[side, j],
            device_id=((up if side == 0 else down), sub),
            device_id_type=MESH,
        )

    def ids_copy(i, origin):
        return pltpu.make_async_remote_copy(
            src_ref=ids_out,
            dst_ref=ids_all.at[z * planes + origin],
            send_sem=ids_send.at[i],
            recv_sem=ids_recv.at[origin],
            device_id=(strip_at(lax.rem(plane + i, planes), z), sub),
            device_id_type=MESH,
        )

    def ids_copy_z(i, origin):
        return pltpu.make_async_remote_copy(
            src_ref=ids_all.at[pl.ds(z * planes, planes)],
            dst_ref=ids_all.at[pl.ds(origin * planes, planes)],
            send_sem=ids_send_z.at[i],
            recv_sem=ids_recv_z.at[origin],
            device_id=(strip_at(plane, lax.rem(z + i, Z)), sub),
            device_id_type=MESH,
        )

    def pair_copy(i, origin):
        other = lax.rem(plane + i, planes)
        return pltpu.make_async_remote_copy(
            src_ref=staging.at[other],
            dst_ref=got.at[origin],
            send_sem=pair_send.at[i],
            recv_sem=pair_recv.at[origin],
            device_id=(strip_at(other, z), sub),
            device_id_type=MESH,
        )

    def pair_copy_z(i, origin):
        other = lax.rem(z + i, Z)
        return pltpu.make_async_remote_copy(
            src_ref=staging_z.at[other],
            dst_ref=got_z.at[origin],
            send_sem=pair_send_z.at[i],
            recv_sem=pair_recv_z.at[origin],
            device_id=(strip_at(plane, other), sub),
            device_id_type=MESH,
        )

    def rows_copy(i, origin):
        return pltpu.make_async_remote_copy(
            src_ref=mine,
            dst_ref=blocks.at[origin],
            send_sem=rows_send.at[i],
            recv_sem=rows_recv.at[origin],
            device_id=(strip, lax.rem(sub + i, subs)),
            device_id_type=MESH,
        )

    def loop(first, last, body, unroll=1):
        def step(i, carry):
            body(i)
            return carry

        lax.fori_loop(first, last, step, 0, unroll=unroll)

    for side in range(2):
        mask_copy(side).start()
    for i in range(1, planes):
        ids_copy(i, plane).start()
    for j in range(2):
        for side in range(2):
            shift(side, j).start()
    ids_all[z * planes + plane] = ids_out[...]

    loads[0].wait()
    for side in range(2):
        mask_copy(side).wait_recv()

    def slot_of(i):
        place = nbr_ids_ref[i // nbrs, i % nbrs] - (strip - 1) * tri
        return jnp.clip(jnp.where(place >= 2 * tri, place - tri, place), 0, 2 * tri - 1)

    zr = lax.broadcasted_iota(jnp.int32, (width, width), 0)
    zc = lax.broadcasted_iota(jnp.int32, (width, width), 1)
    for t in range(tri):
        w = jnp.zeros((width, width), F32)
        factor = jnp.zeros((1, width), F32)
        for n in range(nbrs):
            i = t * nbrs + n
            mask = masks_in[slot_of(i)]
            raw = s_raw[t, n]
            s_mask[i] = (raw.astype(F32) * mask[0:1]).astype(BF16)
            choose = (zc // share == n) & (zr == lax.rem(zc, share) + sub * share)
            w = w + jnp.dot(raw, jnp.where(choose, 1.0, 0.0).astype(BF16), preferred_element_type=F32)
            factor = jnp.where(lane // share == n, mask[1:2] * fock_ref[t, n], factor)
        w_all[t] = (w * factor).astype(BF16)

    def project(j):
        zs = ZS[j]
        for side in range(2):
            shift(side, j).wait_recv()

        def pair(i):
            slot = slot_of(i)
            s = s_mask[i]
            halves = []
            for q in range(zs // 2):
                m = held[j][slot, pl.ds(2 * q, 2)]
                both = jnp.concatenate([m[0], m[1]], axis=1)
                h = jnp.dot(s, both, preferred_element_type=F32).astype(BF16)
                halves += [h[:, :width], h[:, width:]]
            full = jnp.concatenate(halves, axis=0)
            p = lax.dot_general(full, s, (((1,), (1,)), ((), ())), preferred_element_type=F32)
            for q in range(zs):
                pbuf[pl.ds((i * share + Z0[j] + q) * stride, width), :] = p[q * width:(q + 1) * width]

        loop(0, tri * nbrs, pair, unroll=tri * nbrs)

    for i in range(1, planes):
        ids_copy(i, lax.rem(plane + planes - i, planes)).wait_recv()
    for i in range(1, Z):
        ids_copy_z(i, z).start()
    for side in range(2):
        shift(side, 2).start()
    project(0)
    for j in range(3, ZP):
        for side in range(2):
            shift(side, j).start()

    loads[1].wait()
    for i in range(1, Z):
        ids_copy_z(i, lax.rem(z + Z - i, Z)).wait_recv()
    to_smem = pltpu.make_async_copy(ids_all, ids_smem, ids_sem)
    to_smem.start()
    to_smem.wait()

    def stage(m):
        count = jnp.int32(0)
        picks = [jnp.int32(0)] * CAP
        for r in range(wants):
            place = ids_smem[m, 0, r] - strip * owned
            here = (place >= 0) & (place < owned)
            for j in range(CAP):
                picks[j] = jnp.where(here & (count == j), place, picks[j])
            count = count + jnp.where(here, 1, 0)
        for j in range(CAP):
            staging[lax.rem(m, planes), lax.div(m, planes), j] = pairs[picks[j]]

    loop(0, strips, stage)
    for i in range(1, planes):
        pair_copy(i, plane).start()
    got[plane] = staging[plane]
    for j in range(1, ZP):
        project(j)

    def ring(step, e):
        way = lax.rem(e, 2)
        t = e // (2 * AP)
        p = lax.rem(e // 2, AP)
        sign = 1 - 2 * way
        chunk = lax.rem(sub - sign * (1 + step) + 2 * subs, subs)
        a0 = way * (width // 2) + p * rows_p
        return chunk, t, a0, pltpu.make_async_remote_copy(
            src_ref=part.at[t, chunk, pl.ds(a0, rows_p)],
            dst_ref=recv.at[step, t, pl.ds(a0, rows_p)],
            send_sem=ring_send.at[step, e],
            recv_sem=ring_recv.at[step, e],
            device_id=(strip, lax.rem(sub + sign + subs, subs)),
            device_id_type=MESH,
        )

    each = 2 * AP
    pieces = tri * each

    def couple(e):
        chunk, t, a0, copy = ring(0, e)

        def some(i):
            a = a0 + 4 * i
            w = w_all[t][:, :k]
            for v in range(2):
                both = jnp.concatenate(
                    [
                        pbuf[pl.ds(t * k * stride + a + 2 * v + u, k, stride=stride), :].astype(BF16)
                        for u in range(2)
                    ],
                    axis=1,
                )
                o = jnp.dot(w, both, preferred_element_type=F32).astype(BF16)
                for u in range(2):
                    for d in range(subs):
                        part[t, d, a + 2 * v + u] = o[d * share:(d + 1) * share, u * width:(u + 1) * width]

        loop(0, rows_p // 4, some, unroll=rows_p // 4)
        copy.start()

    loop(0, each, couple)
    for i in range(1, planes):
        pair_copy(i, lax.rem(plane + planes - i, planes)).wait_recv()

    def merge(other):
        owners = [lax.div(ids_smem[other * planes + plane, 0, r], owned) for r in range(wants)]
        for r in range(wants):
            rank = jnp.int32(0)
            for q in range(r):
                rank = rank + jnp.where(owners[q] == owners[r], 1, 0)
            source = lax.div(owners[r], Z * CORES) * CORES + lax.rem(owners[r], CORES)
            staging_z[other, r] = got[source, other, jnp.minimum(rank, CAP - 1)]

    loop(0, Z, merge)
    for i in range(1, Z):
        pair_copy_z(i, z).start()
    got_z[z] = staging_z[z]
    loop(each, pieces, couple)

    def onward(step, e):
        _, _, _, before = ring(step - 1, e)
        chunk, t, a0, copy = ring(step, e)
        before.wait_recv()
        rows = pl.ds(a0, rows_p)
        total = part[t, chunk, rows].astype(F32) + recv[step - 1, t, rows].astype(F32)
        part[t, chunk, rows] = total.astype(BF16)
        copy.start()

    for step in range(1, subs - 1):
        loop(0, pieces, functools.partial(onward, step))
        if step == 1:
            for i in range(1, Z):
                pair_copy_z(i, lax.rem(z + Z - i, Z)).wait_recv()
            for r in range(wants):
                owner = lax.div(pair_ids_ref[r // 3, r % 3], owned)
                mine[r] = got_z[lax.rem(lax.div(owner, CORES), Z), r]
            for i in range(1, subs):
                rows_copy(i, sub).start()
            blocks[sub] = mine[...]

    loads[2].wait()
    loads[3].wait()
    for copy in loads[4:]:
        copy.wait()
    for i in range(1, subs):
        rows_copy(i, lax.rem(sub + subs - i, subs)).wait_recv()
    for t in range(tri):
        tno = []
        for r in range(3):
            block = jnp.concatenate([blocks[y, t * 3 + r] for y in range(subs)], axis=0)
            o = over[t, r]
            left = jnp.dot(o, block, preferred_element_type=F32).astype(BF16)
            tno.append(
                lax.dot_general(left, o, (((1,), (1,)), ((), ())), preferred_element_type=F32).astype(BF16)
            )
        tno = jnp.concatenate(tno, axis=1)
        size = size_ref[t]
        live_ab = (zr < size) & (zc < size)
        energy_b = jnp.broadcast_to(energy_rows_ref[t:t + 1], (width, width))
        lmo_total = lmo_ref[triples_ref[t, 0]] + lmo_ref[triples_ref[t, 1]] + lmo_ref[triples_ref[t, 2]]
        den_ab = energy_b.T + energy_b - lmo_total

        def direct(v, t=t, tno=tno, size=size, live_ab=live_ab, den_ab=den_ab):
            both = jnp.concatenate(
                [
                    jnp.concatenate([ints[t, r, 2 * v + u] for r in range(3)], axis=0)
                    for u in range(2)
                ],
                axis=1,
            )
            x = jnp.dot(tno, both, preferred_element_type=F32)
            for u in range(2):
                c = 2 * v + u
                xu = x[:, u * width:(u + 1) * width]
                wsum = xu + xu.T
                live = live_ab & (sub * share + c < size)
                current = amp[t, c].astype(F32)
                den = den_ab + energy_ref[t, sub * share + c]
                scale = 0.7 / den
                base = current - scale * (wsum + den * current)
                at = base_at + (t * share + c) * width
                pbuf[pl.ds(at, width), :] = jnp.where(live, base, 0.0)
                pbuf[pl.ds(flat + at, width), :] = jnp.where(live, scale, 0.0)

        loop(0, share // 2, direct, unroll=4)

    def finish(e):
        _, t, a0, before = ring(subs - 2, e)
        before.wait_recv()

        def some(i):
            for u in range(4):
                a = a0 + 4 * i + u
                total = part[t, sub, a].astype(F32) + recv[subs - 2, t, a].astype(F32)
                pbuf[pl.ds(t * share * stride + a, share, stride=stride), :] = total

        loop(0, rows_p // 4, some, unroll=rows_p // 4)

    def update(t, c):
        at = base_at + (t * share + c) * width
        out_ref[t, c] = (
            pbuf[pl.ds(at, width), :]
            + pbuf[pl.ds(flat + at, width), :] * pbuf[pl.ds((t * share + c) * stride, width), :]
        ).astype(BF16)

    for side in range(2):
        mask_copy(side).wait_send()
        for j in range(ZP):
            shift(side, j).wait_send()
    for i in range(1, planes):
        ids_copy(i, plane).wait_send()
        pair_copy(i, plane).wait_send()
    for i in range(1, Z):
        ids_copy_z(i, z).wait_send()
        pair_copy_z(i, z).wait_send()
    for i in range(1, subs):
        rows_copy(i, sub).wait_send()
    for step in range(subs - 2):
        loop(0, pieces, lambda e: ring(step, e)[3].wait_send())

    for t in range(tri):
        loop(t * each, (t + 1) * each, finish)
        loop(0, share, functools.partial(update, t), unroll=4)
    loop(0, pieces, lambda e: ring(subs - 2, e)[3].wait_send())


def local(
    amplitudes,
    tno_size,
    pair_amps,
    integrals,
    pair_intersection,
    nbr_intersection,
    tno_energy,
    lmo_energy,
    triples,
    pair_ids,
    nbr_ids,
    nbr_fock,
):
    tri, share, width, _ = amplitudes.shape
    nbrs = nbr_ids.shape[1]
    owned = pair_amps.shape[0]
    strips = lax.axis_size("strip")
    subs = lax.axis_size("sub")
    pieces = tri * 2 * AP
    smem = pl.BlockSpec(memory_space=pltpu.SMEM)
    vmem = pl.BlockSpec(memory_space=pltpu.VMEM)
    far = pl.BlockSpec(memory_space=pltpu.HBM)
    dma = pltpu.SemaphoreType.DMA
    return pl.pallas_call(
        functools.partial(kernel, strips, subs, tri, nbrs, share, width, owned),
        out_shape=pltpu.VMEM(amplitudes.shape, BF16),
        in_specs=[smem] * 4 + [far] * 3 + [vmem] + [far] * 5,
        out_specs=vmem,
        scratch_shapes=[
            *[pltpu.VMEM((2 * tri, rows, width, width), BF16) for rows in ZS],
            pltpu.VMEM((tri * nbrs * share * (width + STRIDE_PAD), width), F32),
            pltpu.VMEM((tri, subs, width, share, width), BF16),
            pltpu.VMEM((subs - 1, tri, width, share, width), BF16),
            pltpu.VMEM(integrals.shape, BF16),
            pltpu.VMEM(amplitudes.shape, BF16),
            pltpu.VMEM(pair_amps.shape, BF16),
            pltpu.VMEM(pair_intersection.shape, BF16),
            pltpu.VMEM(nbr_intersection.shape, BF16),
            pltpu.VMEM((tri * nbrs, width, width), BF16),
            pltpu.VMEM((tri, width, width), BF16),
            pltpu.VMEM((tri, 8, width), F32),
            pltpu.VMEM((2 * tri, 8, width), F32),
            pltpu.VMEM((1, width), jnp.int32),
            pltpu.VMEM((strips, 1, width), jnp.int32),
            pltpu.SMEM((strips, 1, width), jnp.int32),
            pltpu.VMEM((strips // Z, Z, CAP, share, width), BF16),
            pltpu.VMEM((strips // Z, Z, CAP, share, width), BF16),
            pltpu.VMEM((Z, tri * 3, share, width), BF16),
            pltpu.VMEM((Z, tri * 3, share, width), BF16),
            pltpu.VMEM((tri * 3, share, width), BF16),
            pltpu.VMEM((subs, tri * 3, share, width), BF16),
            pltpu.SMEM(triples.shape, jnp.int32),
            pltpu.SMEM(lmo_energy.shape, F32),
            pltpu.SMEM(tno_energy.shape, F32),
            dma((8,)),
            dma((2,)),
            dma((2,)),
            dma,
            dma((strips // Z,)),
            dma((strips // Z,)),
            dma((2, ZP)),
            dma((2, ZP)),
            dma((Z,)),
            dma((Z,)),
            dma((strips // Z,)),
            dma((strips // Z,)),
            dma((Z,)),
            dma((Z,)),
            dma((subs,)),
            dma((subs,)),
            dma((subs - 1, pieces)),
            dma((subs - 1, pieces)),
        ],
        compiler_params=pltpu.CompilerParams(
            collective_id=0, has_side_effects=True, vmem_limit_bytes=56 * 1024 * 1024
        ),
    )(
        tno_size, pair_ids, nbr_ids, nbr_fock, triples, lmo_energy, tno_energy,
        tno_energy, amplitudes, pair_amps, integrals, pair_intersection, nbr_intersection,
    )


def solution(mesh):
    in_specs = (
        P("strip", "sub", None, None),
        P("strip"),
        P("strip", "sub", None),
        P("strip", None, "sub", None, None),
        P("strip", None, None, None),
        P("strip", None, None, None),
        P("strip", None),
        P(),
        P("strip", None),
        P("strip", None),
        P("strip", None),
        P("strip", None),
    )
    out_specs = P("strip", "sub", None, None)
    return jax.shard_map(local, mesh=mesh, in_specs=in_specs, out_specs=out_specs, check_vma=False)
```
